32 devices in a mesh: ctx: 8 (over z, x), vis: 4 (over y, core).
Axes of the slice: x: 2, y: 2, z: 4, core: 2. Of those that a mesh axis runs over, the one named last changes fastest.
Arguments:
- features: bfloat16 [8, 256, 1536], P('ctx'), may hold values from -6 to 6
- latent_init: bfloat16 [64, 1536], replicated, may hold values from -6 to 6
- feat_gain: float32 [1536], replicated, may hold values from 0.25 to 1.75
- latent_gain: float32 [1536], replicated, may hold values from 0.25 to 1.75
- resamp_query: bfloat16 [1536, 512], P(None, 'vis'), may hold values from -0.15625 to 0.15625
- resamp_key: bfloat16 [1536, 512], P(None, 'vis'), may hold values from -0.15625 to 0.15625
- resamp_value: bfloat16 [1536, 512], P(None, 'vis'), may hold values from -0.15625 to 0.15625
- resampler_output_weight: bfloat16 [512, 1536], P('vis'), may hold values from -0.25 to 0.25
- cross_key_weight: bfloat16 [1536, 4096], P(None, 'vis'), may hold values from -0.15625 to 0.15625
- cross_value_weight: bfloat16 [1536, 4096], P(None, 'vis'), may hold values from -0.15625 to 0.15625
- slot_image: int32 [8], replicated, may hold values from 0 to 7, each once
- segments: int32 [2048], replicated, may hold values from 0 to 7, as said below
- latest_image: int32 [2048], P('ctx'), may hold values from -1 to 7, as said below
- cross_query: bfloat16 [2048, 4096], P('ctx', 'vis'), may hold values from -6 to 6
- self_query: bfloat16 [2048, 4096], P('ctx', 'vis'), may hold values from -64 to 64
- self_key: bfloat16 [2048, 4096], P('ctx', 'vis'), may hold values from -6 to 6
- self_value: bfloat16 [2048, 4096], P('ctx', 'vis'), may hold values from -6 to 6
- cross_gate: float32 [32], P('vis'), may hold values from 0.3 to 1.5
- grad_output: bfloat16 [2048, 4096], P('ctx', 'vis'), may hold values from -6 to 6
Outputs:
- attended: bfloat16 [2048, 4096], P('ctx', 'vis')
- grad_query: bfloat16 [2048, 4096], P('ctx', 'vis')
- grad_key: bfloat16 [2048, 4096], P('ctx', 'vis')
- grad_value: bfloat16 [2048, 4096], P('ctx', 'vis')
- grad_cross_query: bfloat16 [2048, 4096], P('ctx', 'vis')
- grad_latents: bfloat16 [8, 64, 1536], P('ctx', None, 'vis')
The draws below stay inside these ranges and needn't reach their ends.
Inputs may be any that keep to these rules, and one draw needn't show every extreme that they name: `segments`: documents are numbered in order of position, token 0 begins document 0. `latest_image`: images are numbered in order of position; token 0 has -1.
All inputs are finite; a program needn't handle non-finite values.
Results may differ from the reference program's by a relative error of at most 0.019.
Values may be sent and summed in bfloat16 or wider, within the bound.
A program may use at most 192 MiB of HBM per device.

```python
import math
import jax
import jax.numpy as jnp
from jax import lax

DV = 1536
LATENT_COUNT = 64
FEAT = 256
RESAMPLER_HEADS = 8
RESAMPLER_WIDTH = 64
HEADS = 32
DH = 128
TOKENS = 2048
IMAGE_COUNT = 8
DOCS = 8


def doc_layout(key):
    tail = TOKENS // 8
    first_start = jax.random.randint(jax.random.fold_in(key, 22), (1,), 1, tail + 1).astype(jnp.int32)
    late_starts = (TOKENS - tail + jax.random.permutation(jax.random.fold_in(key, 21), tail)[:DOCS - 2]).astype(jnp.int32)
    starts = jnp.concatenate([first_start, late_starts])
    flags = jnp.zeros((TOKENS,), jnp.int32).at[starts].set(1)
    segment_ids = jnp.cumsum(flags).astype(jnp.int32)
    ranking = jax.random.permutation(jax.random.fold_in(key, 23), TOKENS - 1).astype(jnp.int32)
    positions = jnp.arange(1, TOKENS, dtype=jnp.int32)
    scores = flags[1:] * TOKENS + ranking
    chosen = jnp.argsort(scores, stable=True)[:IMAGE_COUNT]
    image_pos = jnp.sort(positions[chosen]).astype(jnp.int32)
    return (image_pos, segment_ids)


def draw_segments(key, part):
    return doc_layout(key)[1]


def draw_latest_image(key, part):
    image_pos, segment_ids = doc_layout(key)
    flags = jnp.zeros((TOKENS,), jnp.int32).at[image_pos].set(1)
    counted = (jnp.cumsum(flags) - 1).astype(jnp.int32)
    owner_pos = image_pos[jnp.clip(counted, 0, IMAGE_COUNT - 1)]
    same_doc = (counted >= 0) & (segment_ids[owner_pos] == segment_ids)
    return jnp.where(same_doc, counted, -1).astype(jnp.int32)


def key_rows(key):
    return jax.random.truncated_normal(jax.random.fold_in(key, 31), -6.0, 6.0, (TOKENS, HEADS * DH), jnp.float32)


def draw_self_key(key, part):
    rows = key_rows(key)
    return rows.astype(jnp.bfloat16)


def draw_self_query(key, part):
    key = jax.random.fold_in(key, 5)
    fresh = jax.random.truncated_normal(key, -6.0, 6.0, (TOKENS, HEADS * DH), jnp.float32)
    return fresh.astype(jnp.bfloat16)


def level_of(own_key, shape, shards, least, top_value):
    def one(position, blocks):
        draws = jax.random.uniform(jax.random.fold_in(jax.random.fold_in(own_key, 6), position), (blocks,), jnp.float32, least / len(shards), top_value / len(shards))
        return jnp.repeat(jnp.exp(draws), shape[position] // blocks).reshape((-1,) + (1,) * (len(shape) - position - 1))

    level = one(*shards[0])
    for cut in shards[1:]:
        level = level * one(*cut)
    return level


def noise(key, shape, scale, limit, split=(), held_as=jnp.bfloat16):
    factor_of = level_of(key, shape, split, -0.22, 0.18) if split else 1.0
    drawn = jax.random.normal(key, shape, jnp.float32) * scale * factor_of
    return jnp.minimum(jnp.maximum(drawn, -limit), limit).astype(held_as)


def setup_inputs(seed: int = 0) -> dict:
    splits = jax.random.split(jax.random.key(seed), 20)
    return {
        "features": noise(splits[0], (IMAGE_COUNT, FEAT, DV), 1.0, 6.0, ((0, 8),)),
        "latent_init": noise(splits[1], (LATENT_COUNT, DV), 1.0, 6.0),
        "feat_gain": jnp.clip(1.0 + 0.15 * jax.random.normal(splits[2], (DV,), jnp.float32), 0.25, 1.75),
        "latent_gain": jnp.clip(1.0 + 0.15 * jax.random.normal(splits[3], (DV,), jnp.float32), 0.25, 1.75),
        "resamp_query": noise(splits[4], (DV, RESAMPLER_HEADS * RESAMPLER_WIDTH), DV ** -0.5, 0.15625, ((1, 4),)),
        "resamp_key": noise(splits[5], (DV, RESAMPLER_HEADS * RESAMPLER_WIDTH), DV ** -0.5, 0.15625, ((1, 4),)),
        "resamp_value": noise(splits[6], (DV, RESAMPLER_HEADS * RESAMPLER_WIDTH), DV ** -0.5, 0.15625, ((1, 4),)),
        "resampler_output_weight": noise(splits[7], (RESAMPLER_HEADS * RESAMPLER_WIDTH, DV), (RESAMPLER_HEADS * RESAMPLER_WIDTH) ** -0.5, 0.25, ((0, 4),)),
        "cross_key_weight": noise(splits[8], (DV, HEADS * DH), DV ** -0.5, 0.15625, ((1, 4),)),
        "cross_value_weight": noise(splits[9], (DV, HEADS * DH), DV ** -0.5, 0.15625, ((1, 4),)),
        "slot_image": jax.random.permutation(splits[10], IMAGE_COUNT).astype(jnp.int32),
        "segments": draw_segments(jax.random.fold_in(splits[19], 71), 0),
        "latest_image": draw_latest_image(jax.random.fold_in(splits[19], 71), 0),
        "cross_query": noise(splits[13], (TOKENS, HEADS * DH), 1.0, 6.0, ((0, 8), (1, 4))),
        "self_query": draw_self_query(jax.random.fold_in(splits[19], 71), 0),
        "self_key": draw_self_key(jax.random.fold_in(splits[19], 71), 0),
        "self_value": noise(splits[16], (TOKENS, HEADS * DH), 1.0, 6.0, ((0, 8), (1, 4))),
        "cross_gate": jnp.clip(0.3 + 1.2 * jax.random.uniform(splits[17], (HEADS,), jnp.float32) ** level_of(splits[17], (HEADS,), ((0, 4),), -0.2, 0.2), 0.3, 1.5),
        "grad_output": noise(splits[18], (TOKENS, HEADS * DH), 1.0, 6.0, ((0, 8), (1, 4))),
    }


def layer_norm(values, norm_gain):
    center = lax.optimization_barrier(jnp.mean(values, axis=-1, keepdims=True))
    spread = lax.optimization_barrier(jnp.mean((values - center) ** 2, axis=-1, keepdims=True))
    return ((values - center) * lax.rsqrt(spread + 1e-05) * norm_gain).astype(jnp.bfloat16)

def masked_softmax(scores, allowed):
    masked = jnp.where(allowed, scores, jnp.float32(-1e+30))
    peak = lax.optimization_barrier(jnp.max(masked, axis=-1, keepdims=True))
    raised = jnp.where(allowed, jnp.exp(masked - peak), jnp.float32(0.0))
    summed = lax.optimization_barrier(jnp.sum(raised, axis=-1, keepdims=True))
    return raised / jnp.where(summed > 0, summed, jnp.float32(1.0))

def reference(features, latent_init, feat_gain, latent_gain, resamp_query, resamp_key, resamp_value, resampler_output_weight, cross_key_weight, cross_value_weight, slot_image, segments, latest_image, cross_query, self_query, self_key, self_value, cross_gate, grad_output):
    single_float = jnp.float32
    brain_float_half = jnp.bfloat16
    feat_norm = layer_norm(features.astype(single_float), feat_gain)
    lat_norm = layer_norm(latent_init.astype(single_float), latent_gain)
    res_q = jnp.dot(lat_norm, resamp_query, preferred_element_type=single_float).astype(brain_float_half)
    joined = jnp.concatenate([feat_norm, jnp.broadcast_to(lat_norm[None], (IMAGE_COUNT, LATENT_COUNT, DV))], axis=1)
    res_k = jnp.einsum('sfd,de->sfe', joined.astype(single_float), resamp_key.astype(single_float)).astype(brain_float_half)
    res_v = jnp.einsum('sfd,de->sfe', joined.astype(single_float), resamp_value.astype(single_float)).astype(brain_float_half)
    rows = FEAT + LATENT_COUNT
    res_score = jnp.einsum('nhe,sfhe->shnf', res_q.reshape(LATENT_COUNT, RESAMPLER_HEADS, RESAMPLER_WIDTH).astype(single_float), res_k.reshape(IMAGE_COUNT, rows, RESAMPLER_HEADS, RESAMPLER_WIDTH).astype(single_float)) / math.sqrt(RESAMPLER_WIDTH)
    res_prob = jax.nn.softmax(res_score, axis=-1).astype(brain_float_half)
    resampler_mixture = jnp.einsum('shnf,sfhe->snhe', res_prob.astype(single_float), res_v.reshape(IMAGE_COUNT, rows, RESAMPLER_HEADS, RESAMPLER_WIDTH).astype(single_float)).astype(brain_float_half)
    resampler_result = jnp.einsum('uxt,th->uxh', resampler_mixture.reshape(IMAGE_COUNT, LATENT_COUNT, RESAMPLER_HEADS * RESAMPLER_WIDTH).astype(single_float), resampler_output_weight.astype(single_float))
    latent_rows = (latent_init.astype(single_float)[None] + resampler_result).astype(brain_float_half)
    cross_key_rows = jnp.einsum('qzv,vc->qzc', latent_rows.astype(single_float), cross_key_weight.astype(single_float)).astype(brain_float_half)
    cross_value_rows = jnp.einsum('qzv,vc->qzc', latent_rows.astype(single_float), cross_value_weight.astype(single_float)).astype(brain_float_half)
    cross_key_rows = cross_key_rows.reshape(IMAGE_COUNT * LATENT_COUNT, HEADS, DH).transpose(1, 0, 2)
    cross_value_rows = cross_value_rows.reshape(IMAGE_COUNT * LATENT_COUNT, HEADS, DH).transpose(1, 0, 2)
    col_image = jnp.repeat(slot_image, LATENT_COUNT)
    cross_allowed = col_image[None, :] == latest_image[:, None]
    places = jnp.arange(TOKENS)
    self_allowed = (segments[:, None] == segments[None, :]) & (places[None, :] <= places[:, None])
    score_scale = 1.0 / math.sqrt(DH)

    def heads_first(array):
        return array.reshape(TOKENS, HEADS, DH).transpose(1, 0, 2)

    def one_head(inputs):
        query_h, key_h, value_h, cquery_h, grad_h, gate_h, xkey_h, xvalue_h = inputs
        c_prob = masked_softmax(jnp.dot(cquery_h, xkey_h.T, preferred_element_type=single_float) * score_scale, cross_allowed)
        c_half = c_prob.astype(brain_float_half)
        cross = jnp.dot(c_half, xvalue_h, preferred_element_type=single_float)
        gate_tanh = jnp.tanh(gate_h)
        value_in = (value_h.astype(single_float) + gate_tanh * cross).astype(brain_float_half)
        s_prob = masked_softmax(jnp.dot(query_h, key_h.T, preferred_element_type=single_float) * score_scale, self_allowed)
        s_half = s_prob.astype(brain_float_half)
        attended_h = jnp.dot(s_half, value_in, preferred_element_type=single_float).astype(brain_float_half)
        d_prob = jnp.dot(grad_h, value_in.T, preferred_element_type=single_float)
        d_score = (s_prob * (d_prob - lax.optimization_barrier(jnp.sum(s_prob * d_prob, axis=-1, keepdims=True))) * score_scale).astype(brain_float_half)
        grad_query_h = jnp.dot(d_score, key_h, preferred_element_type=single_float).astype(brain_float_half)
        grad_key_h = jnp.dot(d_score.T, query_h, preferred_element_type=single_float).astype(brain_float_half)
        grad_vin = jnp.dot(s_half.T, grad_h, preferred_element_type=single_float)
        d_cross = (gate_tanh * grad_vin).astype(brain_float_half)
        c_dprob = jnp.dot(d_cross, xvalue_h.T, preferred_element_type=single_float)
        c_score = (c_prob * (c_dprob - lax.optimization_barrier(jnp.sum(c_prob * c_dprob, axis=-1, keepdims=True))) * score_scale).astype(brain_float_half)
        grad_cq_h = jnp.dot(c_score, xkey_h, preferred_element_type=single_float).astype(brain_float_half)
        grad_xk = jnp.dot(c_score.T, cquery_h, preferred_element_type=single_float).astype(brain_float_half)
        grad_xv = jnp.dot(c_half.T, d_cross, preferred_element_type=single_float).astype(brain_float_half)
        return (attended_h, grad_query_h, grad_key_h, grad_vin.astype(brain_float_half), grad_cq_h, grad_xk, grad_xv)
    results = lax.map(one_head, (heads_first(self_query), heads_first(self_key), heads_first(self_value), heads_first(cross_query), heads_first(grad_output), cross_gate, cross_key_rows, cross_value_rows))

    def tokens_first(array):
        return array.transpose(1, 0, 2).reshape(TOKENS, HEADS * DH)
    attended, grad_query, grad_key, grad_value, grad_cross_query, grad_xk, grad_xv = results
    flat_k = grad_xk.transpose(1, 0, 2).reshape(IMAGE_COUNT * LATENT_COUNT, HEADS * DH)
    flat_v = grad_xv.transpose(1, 0, 2).reshape(IMAGE_COUNT * LATENT_COUNT, HEADS * DH)
    grad_latents = jnp.dot(flat_k, cross_key_weight.T, preferred_element_type=single_float) + jnp.dot(flat_v, cross_value_weight.T, preferred_element_type=single_float)
    grad_latents = grad_latents.astype(brain_float_half).reshape(IMAGE_COUNT, LATENT_COUNT, DV)
    return (tokens_first(attended), tokens_first(grad_query), tokens_first(grad_key), tokens_first(grad_value), tokens_first(grad_cross_query), grad_latents)
```

```python
import functools
import math

import jax
import jax.numpy as jnp
from jax import lax
from jax.experimental import pallas as pl
from jax.experimental.pallas import tpu as pltpu
from jax.sharding import PartitionSpec as P

LATENT_COUNT = 64
RESAMPLER_WIDTH = 64
DH = 128


def layer_norm(values, norm_gain):
    center = jnp.mean(values, axis=-1, keepdims=True)
    spread = jnp.mean((values - center) ** 2, axis=-1, keepdims=True)
    return ((values - center) * lax.rsqrt(spread + 1e-05) * norm_gain).astype(jnp.bfloat16)


def masked_softmax(scores, allowed):
    masked = jnp.where(allowed, scores, jnp.float32(-1e30))
    peak = jnp.max(masked, axis=-1, keepdims=True)
    raised = jnp.where(allowed, jnp.exp(masked - peak), jnp.float32(0.0))
    summed = jnp.sum(raised, axis=-1, keepdims=True)
    return raised / jnp.where(summed > 0, summed, jnp.float32(1.0))


def shards(
    features,
    latent_init,
    feat_gain,
    latent_gain,
    resamp_query,
    resamp_key,
    resamp_value,
    resampler_output_weight,
    cross_key_weight,
    cross_value_weight,
    slot_image,
    segments,
    latest_image,
    cross_query,
    self_query,
    self_key,
    self_value,
    cross_gate,
    grad_output,
):
    single_float = jnp.float32
    brain_float_half = jnp.bfloat16
    shard_at = lax.axis_index("ctx")
    local_rows = self_query.shape[0]
    head_columns = self_query.shape[1]
    local_heads = cross_gate.shape[0]
    score_scale = 1.0 / math.sqrt(DH)
    slots_here = features.shape[0]
    feat_rows = features.shape[1]
    feat_norm = layer_norm(features.astype(single_float), feat_gain)
    lat_norm = layer_norm(latent_init.astype(single_float), latent_gain)
    res_heads = resamp_query.shape[1] // RESAMPLER_WIDTH
    res_q = jnp.dot(lat_norm, resamp_query, preferred_element_type=single_float).astype(
        brain_float_half
    )
    joined = jnp.concatenate([feat_norm, lat_norm[None]], axis=1)
    res_k = jnp.einsum(
        "sfd,de->sfe", joined, resamp_key, preferred_element_type=single_float
    ).astype(brain_float_half)
    res_v = jnp.einsum(
        "sfd,de->sfe", joined, resamp_value, preferred_element_type=single_float
    ).astype(brain_float_half)
    joined_rows = feat_rows + LATENT_COUNT
    res_score = jnp.einsum(
        "nhe,sfhe->shnf",
        res_q.reshape(LATENT_COUNT, res_heads, RESAMPLER_WIDTH),
        res_k.reshape(slots_here, joined_rows, res_heads, RESAMPLER_WIDTH),
        preferred_element_type=single_float,
    ) / math.sqrt(RESAMPLER_WIDTH)
    res_prob = jax.nn.softmax(res_score, axis=-1).astype(brain_float_half)
    resampler_mixture = jnp.einsum(
        "shnf,sfhe->snhe",
        res_prob,
        res_v.reshape(slots_here, joined_rows, res_heads, RESAMPLER_WIDTH),
        preferred_element_type=single_float,
    ).astype(brain_float_half)
    partial_out = jnp.einsum(
        "uxt,th->uxh",
        resampler_mixture.reshape(slots_here, LATENT_COUNT, res_heads * RESAMPLER_WIDTH),
        resampler_output_weight,
        preferred_element_type=single_float,
    )
    resampled = lax.psum(partial_out, "vis")
    latent_rows = (latent_init.astype(single_float)[None] + resampled).astype(brain_float_half)
    latent_stack = lax.all_gather(latent_rows, "ctx", axis=0, tiled=True)
    cross_key_rows = jnp.einsum(
        "qzv,vc->qzc", latent_stack, cross_key_weight, preferred_element_type=single_float
    ).astype(brain_float_half)
    cross_value_rows = jnp.einsum(
        "qzv,vc->qzc", latent_stack, cross_value_weight, preferred_element_type=single_float
    ).astype(brain_float_half)
    all_slots = cross_key_rows.shape[0]
    key_count = all_slots * LATENT_COUNT
    xkey_rows = cross_key_rows.reshape(key_count, local_heads, DH)
    xvalue_rows = cross_value_rows.reshape(key_count, local_heads, DH)
    col_image = jnp.repeat(slot_image, LATENT_COUNT)
    cquery_rows = cross_query.reshape(local_rows, local_heads, DH)
    cross_allowed = (col_image[None, :] == latest_image[:, None])[None]
    c_prob = masked_softmax(
        jnp.einsum("thd,khd->htk", cquery_rows, xkey_rows, preferred_element_type=single_float)
        * score_scale,
        cross_allowed,
    )
    c_half = c_prob.astype(brain_float_half)
    cross = jnp.einsum("htk,khd->thd", c_half, xvalue_rows, preferred_element_type=single_float)
    gate_tanh = jnp.tanh(cross_gate)[None, :, None]
    value_in = (
        self_value.reshape(local_rows, local_heads, DH).astype(single_float) + gate_tanh * cross
    ).astype(brain_float_half)
    keys_all, values_all = (
        lax.all_gather(self_key, "ctx", axis=0, tiled=True),
        lax.all_gather(value_in.reshape(local_rows, head_columns), "ctx", axis=0, tiled=True),
    )
    total_rows = keys_all.shape[0]
    keys_all = keys_all.reshape(total_rows, local_heads, DH)
    values_all = values_all.reshape(total_rows, local_heads, DH)
    query_rows = self_query.reshape(local_rows, local_heads, DH)
    grad_rows = grad_output.reshape(local_rows, local_heads, DH)
    query_pos = shard_at * local_rows + jnp.arange(local_rows, dtype=jnp.int32)
    key_pos = jnp.arange(total_rows, dtype=jnp.int32)
    query_seg = lax.dynamic_slice_in_dim(segments, shard_at * local_rows, local_rows, 0)
    self_allowed = (
        (query_seg[:, None] == segments[None, :]) & (key_pos[None, :] <= query_pos[:, None])
    )[None]
    self_score = (
        jnp.einsum("thd,khd->htk", query_rows, keys_all, preferred_element_type=single_float)
        * score_scale
    )
    s_prob = masked_softmax(self_score, self_allowed)
    s_half = s_prob.astype(brain_float_half)
    attended = (
        jnp.einsum("htk,khd->thd", s_half, values_all, preferred_element_type=single_float)
        .astype(brain_float_half)
        .reshape(local_rows, head_columns)
    )
    d_prob = jnp.einsum("thd,khd->htk", grad_rows, values_all, preferred_element_type=single_float)
    row_delta = jnp.sum(s_prob * d_prob, axis=-1)
    d_score = (s_prob * (d_prob - row_delta[..., None]) * score_scale).astype(brain_float_half)
    grad_query = (
        jnp.einsum("htk,khd->thd", d_score, keys_all, preferred_element_type=single_float)
        .astype(brain_float_half)
        .reshape(local_rows, head_columns)
    )
    masked_score = jnp.where(self_allowed, self_score, single_float(-1e30))
    row_peak = jnp.max(masked_score, axis=-1)
    row_total = jnp.sum(
        jnp.where(self_allowed, jnp.exp(masked_score - row_peak[..., None]), single_float(0.0)),
        axis=-1,
    )
    log_total = row_peak + jnp.log(row_total)
    query_all, grad_all = (
        lax.all_gather(self_query, "ctx", axis=0, tiled=True),
        lax.all_gather(grad_output, "ctx", axis=0, tiled=True),
    )
    lse_all, delta_all = (
        lax.all_gather(log_total.T, "ctx", axis=0, tiled=True),
        lax.all_gather(row_delta.T, "ctx", axis=0, tiled=True),
    )
    query_all = query_all.reshape(total_rows, local_heads, DH)
    grad_all = grad_all.reshape(total_rows, local_heads, DH)
    own_keys = self_key.reshape(local_rows, local_heads, DH)
    owned_allowed = (
        (segments[:, None] == query_seg[None, :]) & (query_pos[None, :] <= key_pos[:, None])
    )[None]
    back_score = (
        jnp.einsum("qhd,khd->hqk", query_all, own_keys, preferred_element_type=single_float)
        * score_scale
    )
    back_prob = jnp.exp(
        jnp.where(owned_allowed, back_score - lse_all.T[:, :, None], single_float(-1e30))
    )
    back_prob = jnp.where(owned_allowed, back_prob, single_float(0.0))
    back_half = back_prob.astype(brain_float_half)
    back_dprob = jnp.einsum("qhd,khd->hqk", grad_all, value_in, preferred_element_type=single_float)
    back_dscore = (back_prob * (back_dprob - delta_all.T[:, :, None]) * score_scale).astype(
        brain_float_half
    )
    key_sum = jnp.einsum(
        "hqk,qhd->khd", back_dscore, query_all, preferred_element_type=single_float
    ).reshape(local_rows, head_columns)
    vin_sum = jnp.einsum(
        "hqk,qhd->khd", back_half, grad_all, preferred_element_type=single_float
    ).reshape(local_rows, head_columns)
    grad_key = key_sum.astype(brain_float_half)
    grad_value = vin_sum.astype(brain_float_half)
    d_cross = (gate_tanh * vin_sum.reshape(local_rows, local_heads, DH)).astype(brain_float_half)
    c_dprob = jnp.einsum("thd,khd->htk", d_cross, xvalue_rows, preferred_element_type=single_float)
    c_score = (
        c_prob * (c_dprob - jnp.sum(c_prob * c_dprob, axis=-1, keepdims=True)) * score_scale
    ).astype(brain_float_half)
    grad_cross_query = (
        jnp.einsum("htk,khd->thd", c_score, xkey_rows, preferred_element_type=single_float)
        .astype(brain_float_half)
        .reshape(local_rows, head_columns)
    )
    grad_xk = jnp.einsum("htk,thd->khd", c_score, cquery_rows, preferred_element_type=single_float)
    grad_xv = jnp.einsum("htk,thd->khd", c_half, d_cross, preferred_element_type=single_float)
    stacked = jnp.concatenate(
        [
            grad_xk.reshape(all_slots, LATENT_COUNT, head_columns),
            grad_xv.reshape(all_slots, LATENT_COUNT, head_columns),
        ],
        axis=2,
    )
    local_gradients = lax.psum_scatter(stacked, "ctx", scatter_dimension=0, tiled=True).astype(
        brain_float_half
    )
    latent_part = jnp.einsum(
        "zmx,tx->zmt",
        local_gradients[:, :, :head_columns],
        cross_key_weight,
        preferred_element_type=single_float,
    )
    latent_part = latent_part + jnp.einsum(
        "zmx,tx->zmt",
        local_gradients[:, :, head_columns:],
        cross_value_weight,
        preferred_element_type=single_float,
    )
    grad_latents = lax.psum_scatter(latent_part, "vis", scatter_dimension=2, tiled=True).astype(
        brain_float_half
    )
    return (attended, grad_query, grad_key, grad_value, grad_cross_query, grad_latents)


F32 = jnp.float32
BF16 = jnp.bfloat16
MASKED = -1e30


def mm(a, b):
    return lax.dot_general(a, b, (((1,), (0,)), ((), ())), preferred_element_type=F32)


def mm_nt(a, b):
    return lax.dot_general(a, b, (((1,), (1,)), ((), ())), preferred_element_type=F32)


def mm_tn(a, b):
    return lax.dot_general(a, b, (((0,), (0,)), ((), ())), preferred_element_type=F32)


def normed(values, norm_gain):
    v = values.astype(F32)
    center = jnp.mean(v, axis=-1, keepdims=True)
    spread = jnp.mean((v - center) ** 2, axis=-1, keepdims=True)
    return ((v - center) * lax.rsqrt(spread + 1e-05) * norm_gain).astype(BF16)


def head_kernel(
    nc,
    nv,
    feat,
    lat0,
    fgain,
    lgain,
    wq,
    wk,
    wv,
    wo,
    xwk,
    xwv,
    img_row,
    seg_row,
    seg_col,
    latest,
    gate,
    cq_in,
    q_in,
    k_in,
    v_in,
    g_in,
    att_out,
    gq_out,
    gk_out,
    gv_out,
    gcq_out,
    glat_out,
    cq,
    q,
    k,
    v,
    g,
    wxk,
    wxv,
    lat_rows,
    lat_col,
    part,
    part_in,
    lat_mine,
    lat_all,
    xk_loc,
    xv_loc,
    xk,
    xv,
    vin,
    cprob,
    s_buf,
    dp_buf,
    dk,
    dv,
    att_s,
    gq_s,
    gk_s,
    gv_s,
    gcq_s,
    gxk,
    gxv,
    gxk_s,
    gxv_s,
    own_k,
    own_v,
    lpart,
    lpart_in,
    w_sem,
    own_sem,
    in_send,
    in_recv,
    lat_send,
    lat_recv,
    p_send,
    p_recv,
    l_send,
    l_recv,
    x_send,
    x_recv,
    o_own,
    o_send,
    o_recv,
    gx_send,
    gx_recv,
    r_send,
    r_recv,
):
    me = lax.axis_index("ctx")
    vi = lax.axis_index("vis")
    rows = q_in.shape[0]
    total = rows * nc
    slots = lat0.shape[0]
    wide = lat0.shape[1]
    cut = wide // nv
    scale = 1.0 / math.sqrt(DH)
    MESH = pl.DeviceIdType.MESH

    def remote(s, d, ss, rs, c, w):
        return pltpu.make_async_remote_copy(
            src_ref=s, dst_ref=d, send_sem=ss, recv_sem=rs, device_id=(c, w), device_id_type=MESH
        )

    barrier = pltpu.get_barrier_semaphore()
    for o in range(1, nc):
        pl.semaphore_signal(barrier, inc=1, device_id=(lax.rem(me + o, nc), vi), device_id_type=MESH)
    for o in range(1, nv):
        pl.semaphore_signal(barrier, inc=1, device_id=(me, lax.rem(vi + o, nv)), device_id_type=MESH)
    pl.semaphore_wait(barrier, nc + nv - 2)

    def head_of(p):
        return pl.ds(pl.multiple_of(p * DH, DH), DH)

    def rows_of(p):
        return pl.ds(pl.multiple_of(p * rows, rows), rows)

    def slot_of(p):
        return pl.ds(pl.multiple_of(p * slots, slots), slots)

    def cut_of(p):
        return pl.ds(pl.multiple_of(p * cut, cut), cut)

    ins = ((cq_in, cq), (v_in, v), (q_in, q), (k_in, k), (g_in, g))

    def in_copy(a, p):
        return remote(
            ins[a][0].at[:, head_of(p)], ins[a][1].at[rows_of(me), :],
            in_send.at[a, p], in_recv.at[a, me], p, vi,
        )

    def in_wait(a, p):
        return remote(
            ins[a][0].at[:, head_of(p)], ins[a][1].at[rows_of(p), :],
            in_send.at[a, p], in_recv.at[a, p], p, vi,
        )

    def lat_copy(p):
        return remote(latest, lat_rows.at[me], lat_send.at[p], lat_recv.at[me], p, vi)

    def lat_wait(p):
        return remote(latest, lat_rows.at[p], lat_send.at[p], lat_recv.at[p], p, vi)

    def peers(fn):
        def step(o, c):
            fn(lax.rem(me + o, nc))
            return c

        lax.fori_loop(1, nc, step, 0)

    def mates(fn):
        for o in range(1, nv):
            fn(lax.rem(vi + o, nv))

    wcopies = (
        pltpu.make_async_copy(xwk, wxk, w_sem.at[0]),
        pltpu.make_async_copy(xwv, wxv, w_sem.at[1]),
    )
    for c in wcopies:
        c.start()

    def start_in(p):
        lat_copy(p).start()
        for a in range(5):
            in_copy(a, p).start()

    peers(start_in)
    owns = tuple(
        pltpu.make_async_copy(s.at[:, head_of(me)], d.at[rows_of(me), :], own_sem.at[a])
        for a, (s, d) in enumerate(ins)
    )
    for c in owns:
        c.start()
    lat_rows[me] = latest[...]

    f_norm = normed(feat[0], fgain[...])
    l_norm = normed(lat0[...], lgain[...])
    rq = mm(l_norm, wq[...]).astype(BF16)
    rkf = mm(f_norm, wk[...]).astype(BF16)
    rkl = mm(l_norm, wk[...]).astype(BF16)
    rvf = mm(f_norm, wv[...]).astype(BF16)
    rvl = mm(l_norm, wv[...]).astype(BF16)
    width = rq.shape[1]
    lane = lax.broadcasted_iota(jnp.int32, (1, width), 1)
    mix = jnp.zeros((slots, width), F32)
    r_scale = 1.0 / math.sqrt(RESAMPLER_WIDTH)
    for h in range(width // RESAMPLER_WIDTH):
        inside = (lane >= h * RESAMPLER_WIDTH) & (lane < (h + 1) * RESAMPLER_WIDTH)
        qh = jnp.where(inside, rq, jnp.zeros_like(rq))
        sf = mm_nt(qh, rkf) * r_scale
        sl = mm_nt(qh, rkl) * r_scale
        peak = jnp.maximum(jnp.max(sf, axis=-1, keepdims=True), jnp.max(sl, axis=-1, keepdims=True))
        ef, el = jnp.exp(sf - peak), jnp.exp(sl - peak)
        inv = 1.0 / (jnp.sum(ef, axis=-1, keepdims=True) + jnp.sum(el, axis=-1, keepdims=True))
        mh = mm((ef * inv).astype(BF16), rvf) + mm((el * inv).astype(BF16), rvl)
        mix = jnp.where(inside, mh, mix)
    part[...] = mm(mix.astype(BF16), wo[...])

    def p_copy(w):
        return remote(part.at[:, cut_of(w)], part_in.at[vi], p_send.at[w], p_recv.at[vi], me, w)

    def p_wait(w):
        return remote(part.at[:, cut_of(w)], part_in.at[w], p_send.at[w], p_recv.at[w], me, w)

    mates(lambda w: p_copy(w).start())
    part_in[vi] = part[:, cut_of(vi)]
    mates(lambda w: p_wait(w).wait_recv())
    summed = part_in[0]
    for w in range(1, nv):
        summed = summed + part_in[w]
    lat_mine[...] = (lat0[:, cut_of(vi)].astype(F32) + summed).astype(BF16)

    def l_copy(w):
        return remote(lat_mine, lat_all.at[vi], l_send.at[w], l_recv.at[vi], me, w)

    def l_wait(w):
        return remote(lat_mine, lat_all.at[w], l_send.at[w], l_recv.at[w], me, w)

    mates(lambda w: l_copy(w).start())
    lat_all[vi] = lat_mine[...]
    for c in wcopies:
        c.wait()
    mates(lambda w: l_wait(w).wait_recv())
    for wx, loc in ((wxk, xk_loc), (wxv, xv_loc)):
        acc = mm(lat_all[0], wx[0:cut, :])
        for w in range(1, nv):
            acc = acc + mm(lat_all[w], wx[w * cut : (w + 1) * cut, :])
        loc[...] = acc.astype(BF16)

    xs = ((xk_loc, xk), (xv_loc, xv))

    def x_copy(a, p):
        return remote(
            xs[a][0].at[:, head_of(p)], xs[a][1].at[slot_of(me), :],
            x_send.at[a, p], x_recv.at[a, me], p, vi,
        )

    def x_wait(a, p):
        return remote(
            xs[a][0].at[:, head_of(p)], xs[a][1].at[slot_of(p), :],
            x_send.at[a, p], x_recv.at[a, p], p, vi,
        )

    peers(lambda p: (x_copy(0, p).start(), x_copy(1, p).start()))
    xk[slot_of(me), :] = xk_loc[:, head_of(me)]
    xv[slot_of(me), :] = xv_loc[:, head_of(me)]

    peers(lambda p: lat_wait(p).wait_recv())
    for p in range(nc):
        for c in range(rows // 128):
            line = lat_rows[p, 0:1, c * 128 : (c + 1) * 128]
            lat_col[p * rows + c * 128 : p * rows + (c + 1) * 128, :] = jnp.broadcast_to(
                line, (128, 128)
            ).T

    peers(lambda p: (x_wait(0, p).wait_recv(), x_wait(1, p).wait_recv()))
    for c in owns:
        c.wait()

    def wait_in(p):
        for a in range(5):
            in_wait(a, p).wait_recv()

    peers(wait_in)

    images = img_row[0:1, :]
    gate_h = gate[0:1, 0:1]

    def cross_step(i, carry):
        r = rows_of(i)
        allowed = images == lat_col[r, 0:1]
        s = jnp.where(allowed, mm_nt(cq[r, :], xk[...]) * scale, MASKED)
        peak = jnp.max(s, axis=-1, keepdims=True)
        e = jnp.where(allowed, jnp.exp(s - peak), 0.0)
        tot = jnp.sum(e, axis=-1, keepdims=True)
        p = e / jnp.where(tot > 0, tot, 1.0)
        cprob[r, :] = p
        crossed = mm(p.astype(BF16), xv[...])
        vin[r, :] = (v[r, :].astype(F32) + gate_h * crossed).astype(BF16)
        return carry

    lax.fori_loop(0, nc, cross_step, 0)

    dk[...] = jnp.zeros_like(dk)
    dv[...] = jnp.zeros_like(dv)
    gxk[...] = jnp.zeros_like(gxk)
    gxv[...] = jnp.zeros_like(gxv)
    kc = 2 * rows

    def key_cols(j):
        return pl.ds(pl.multiple_of(j * kc, kc), kc)

    outs = ((att_s, att_out), (gq_s, gq_out), (gk_s, gk_out), (gv_s, gv_out), (gcq_s, gcq_out))

    def o_copy(a, p):
        return remote(
            outs[a][0].at[rows_of(p), :], outs[a][1].at[:, head_of(me)],
            o_send.at[a, p], o_recv.at[a, me], p, vi,
        )

    def o_wait(a, p):
        return remote(
            outs[a][0].at[rows_of(p), :], outs[a][1].at[:, head_of(p)],
            o_send.at[a, p], o_recv.at[a, p], p, vi,
        )

    def o_local(a):
        return pltpu.make_async_copy(
            outs[a][0].at[rows_of(me), :], outs[a][1].at[:, head_of(me)], o_own.at[a]
        )

    def self_step(b, carry):
        i = nc - 1 - b
        r = rows_of(i)
        chunks = i // 2 + 1
        qi, gi = q[r, :], g[r, :]
        seg_i = seg_col[r, 0:1]
        q_pos = i * rows + lax.broadcasted_iota(jnp.int32, (rows, kc), 0)
        k_iota = lax.broadcasted_iota(jnp.int32, (rows, kc), 1)

        def lanes(x, op):
            out = x[:, 0:128]
            for c in range(1, kc // 128):
                out = op(out, x[:, c * 128 : (c + 1) * 128])
            return out

        def pass1(j, m):
            cols = key_cols(j)
            allowed = (seg_row[0:1, cols] == seg_i) & (j * kc + k_iota <= q_pos)
            s = jnp.where(allowed, mm_nt(qi, k[cols, :]) * scale, MASKED)
            s_buf[:, cols] = s
            return jnp.maximum(m, lanes(s, jnp.maximum))

        m = lax.fori_loop(0, chunks, pass1, jnp.full((rows, 128), MASKED, F32))
        m = jnp.max(m, axis=-1, keepdims=True)

        def pass2(j, c):
            tot, dl, acc = c
            cols = key_cols(j)
            p = jnp.exp(s_buf[:, cols] - m)
            s_buf[:, cols] = p
            vj = vin[cols, :]
            dp = mm_nt(gi, vj)
            dp_buf[:, cols] = dp
            return tot + lanes(p, jnp.add), dl + lanes(p * dp, jnp.add), acc + mm(p.astype(BF16), vj)

        zero = jnp.zeros((rows, 128), F32)
        tot, dl, acc = lax.fori_loop(0, chunks, pass2, (zero, zero, zero))
        inv = 1.0 / jnp.sum(tot, axis=-1, keepdims=True)
        delta = jnp.sum(dl, axis=-1, keepdims=True) * inv
        att_s[r, :] = (acc * inv).astype(BF16)

        def pass3(j, acc):
            cols = key_cols(j)
            p = s_buf[:, cols] * inv
            ds = (p * (dp_buf[:, cols] - delta) * scale).astype(BF16)
            dk[cols, :] += mm_tn(ds, qi)
            dv[cols, :] += mm_tn(p.astype(BF16), gi)
            return acc + mm(ds, k[cols, :])

        gq_s[r, :] = lax.fori_loop(0, chunks, pass3, zero).astype(BF16)
        dvi = dv[r, :]
        gk_s[r, :] = dk[r, :].astype(BF16)
        gv_s[r, :] = dvi.astype(BF16)

        dc = (gate_h * dvi).astype(BF16)
        cp = cprob[r, :]
        cd = mm_nt(dc, xv[...])
        cs = (cp * (cd - jnp.sum(cp * cd, axis=-1, keepdims=True)) * scale).astype(BF16)
        gcq_s[r, :] = mm(cs, xk[...]).astype(BF16)
        gxk[...] += mm_tn(cs, cq[r, :])
        gxv[...] += mm_tn(cp.astype(BF16), dc)

        @pl.when(i != me)
        def _():
            for a in range(5):
                o_copy(a, i).start()

        @pl.when(i == me)
        def _():
            for a in range(5):
                o_local(a).start()

        return carry

    lax.fori_loop(0, nc, self_step, 0)

    gxk_s[...] = gxk[...].astype(BF16)
    gxv_s[...] = gxv[...].astype(BF16)
    gxs = ((gxk_s, own_k), (gxv_s, own_v))

    def gx_copy(a, p):
        return remote(
            gxs[a][0].at[slot_of(p), :], gxs[a][1].at[:, head_of(me)],
            gx_send.at[a, p], gx_recv.at[a, me], p, vi,
        )

    def gx_wait(a, p):
        return remote(
            gxs[a][0].at[slot_of(p), :], gxs[a][1].at[:, head_of(p)],
            gx_send.at[a, p], gx_recv.at[a, p], p, vi,
        )

    peers(lambda p: (gx_copy(0, p).start(), gx_copy(1, p).start()))
    own_k[:, head_of(me)] = gxk_s[slot_of(me), :]
    own_v[:, head_of(me)] = gxv_s[slot_of(me), :]
    peers(lambda p: (gx_wait(0, p).wait_recv(), gx_wait(1, p).wait_recv()))
    lpart[...] = mm_nt(own_k[...], wxk[...]) + mm_nt(own_v[...], wxv[...])

    def r_copy(w):
        return remote(lpart.at[:, cut_of(w)], lpart_in.at[vi], r_send.at[w], r_recv.at[vi], me, w)

    def r_wait(w):
        return remote(lpart.at[:, cut_of(w)], lpart_in.at[w], r_send.at[w], r_recv.at[w], me, w)

    mates(lambda w: r_copy(w).start())
    lpart_in[vi] = lpart[:, cut_of(vi)]
    mates(lambda w: r_wait(w).wait_recv())
    summed = lpart_in[0]
    for w in range(1, nv):
        summed = summed + lpart_in[w]
    glat_out[0] = summed.astype(BF16)

    def finish(p):
        lat_wait(p).wait_send()
        for a in range(5):
            in_wait(a, p).wait_send()
            o_wait(a, p).wait()
        for a in range(2):
            x_wait(a, p).wait_send()
            gx_wait(a, p).wait_send()

    peers(finish)

    def finish_mate(w):
        p_wait(w).wait_send()
        l_wait(w).wait_send()
        r_wait(w).wait_send()

    mates(finish_mate)
    for a in range(5):
        o_local(a).wait()


def by_head(nc, nv, *args):
    (feat, lat0, fgain, lgain, wq, wk, wv, wo, xwk, xwv, slot_image, segments, latest_image,
     cross_query, self_query, self_key, self_value, cross_gate, grad_output) = args
    rows, cols = self_query.shape
    total = rows * nc
    slots, wide = lat0.shape
    xrows = nc * slots
    cut = wide // nv
    gate = jnp.tanh(lax.dynamic_slice_in_dim(cross_gate, lax.axis_index("ctx"), 1, 0))
    gate = jnp.broadcast_to(gate[None], (8, 128))
    img_row = jnp.broadcast_to(jnp.repeat(slot_image, slots).astype(F32)[None], (8, xrows))
    seg_row = jnp.broadcast_to(segments[None], (8, total))
    seg_col = jnp.broadcast_to(segments[:, None], (total, 128))
    latest = jnp.broadcast_to(latest_image.astype(F32)[None], (8, rows))
    vmem = pl.BlockSpec(memory_space=pltpu.VMEM)
    hbm = pl.BlockSpec(memory_space=pl.ANY)
    tok = jax.ShapeDtypeStruct((rows, cols), BF16)
    V = pltpu.VMEM
    dma = pltpu.SemaphoreType.DMA
    scratch = (
        [V((total, DH), BF16)] * 5
        + [V((wide, cols), BF16)] * 2
        + [V((nc, 8, rows), F32), V((total, 128), F32)]
        + [V((slots, wide), F32), V((nv, slots, cut), F32)]
        + [V((slots, cut), BF16), V((nv, slots, cut), BF16)]
        + [V((slots, cols), BF16)] * 2
        + [V((xrows, DH), BF16)] * 2
        + [V((total, DH), BF16), V((total, xrows), F32)]
        + [V((rows, total), F32)] * 2
        + [V((total, DH), F32)] * 2
        + [V((total, DH), BF16)] * 5
        + [V((xrows, DH), F32)] * 2
        + [V((xrows, DH), BF16)] * 2
        + [V((slots, cols), BF16)] * 2
        + [V((slots, wide), F32), V((nv, slots, cut), F32)]
        + [dma((2,)), dma((5,))]
        + [dma((5, nc))] * 2
        + [dma((nc,))] * 2
        + [dma((nv,))] * 4
        + [dma((2, nc))] * 2
        + [dma((5,))]
        + [dma((5, nc))] * 2
        + [dma((2, nc))] * 2
        + [dma((nv,))] * 2
    )
    return pl.pallas_call(
        functools.partial(head_kernel, nc, nv),
        out_shape=[tok] * 5 + [jax.ShapeDtypeStruct((1, slots, cut), BF16)],
        in_specs=[vmem] * 8 + [hbm] * 2 + [vmem] * 5 + [hbm] * 5,
        out_specs=[hbm] * 5 + [vmem],
        scratch_shapes=scratch,
        compiler_params=pltpu.CompilerParams(
            collective_id=0, has_side_effects=True, vmem_limit_bytes=52 * 1024 * 1024
        ),
        name="head_window",
    )(feat, lat0, fgain[None], lgain[None], wq, wk, wv, wo, xwk, xwv, img_row, seg_row, seg_col,
      latest, gate, cross_query, self_query, self_key, self_value, grad_output)


def dispatch(nc, nv, *args):
    if args[17].shape[0] == nc and args[0].shape[0] == 1:
        return tuple(by_head(nc, nv, *args))
    return shards(*args)


def solution(mesh):
    in_specs = (
        P("ctx", None, None),
        P(),
        P(),
        P(),
        P(None, "vis"),
        P(None, "vis"),
        P(None, "vis"),
        P("vis", None),
        P(None, "vis"),
        P(None, "vis"),
        P(),
        P(),
        P("ctx"),
        P("ctx", "vis"),
        P("ctx", "vis"),
        P("ctx", "vis"),
        P("ctx", "vis"),
        P("vis"),
        P("ctx", "vis"),
    )
    out_specs = (
        P("ctx", "vis"),
        P("ctx", "vis"),
        P("ctx", "vis"),
        P("ctx", "vis"),
        P("ctx", "vis"),
        P("ctx", None, "vis"),
    )
    body = functools.partial(dispatch, mesh.shape["ctx"], mesh.shape["vis"])
    return jax.shard_map(body, mesh=mesh, in_specs=in_specs, out_specs=out_specs, check_vma=False)
```

```python
import functools
import math

import jax
import jax.numpy as jnp
from jax import lax
from jax.experimental import pallas as pl
from jax.experimental.pallas import tpu as pltpu
from jax.sharding import PartitionSpec as P

LATENT_COUNT = 64
RESAMPLER_WIDTH = 64
DH = 128


def layer_norm(values, norm_gain):
    center = jnp.mean(values, axis=-1, keepdims=True)
    spread = jnp.mean((values - center) ** 2, axis=-1, keepdims=True)
    return ((values - center) * lax.rsqrt(spread + 1e-05) * norm_gain).astype(jnp.bfloat16)


def masked_softmax(scores, allowed):
    masked = jnp.where(allowed, scores, jnp.float32(-1e30))
    peak = jnp.max(masked, axis=-1, keepdims=True)
    raised = jnp.where(allowed, jnp.exp(masked - peak), jnp.float32(0.0))
    summed = jnp.sum(raised, axis=-1, keepdims=True)
    return raised / jnp.where(summed > 0, summed, jnp.float32(1.0))


def shards(
    features,
    latent_init,
    feat_gain,
    latent_gain,
    resamp_query,
    resamp_key,
    resamp_value,
    resampler_output_weight,
    cross_key_weight,
    cross_value_weight,
    slot_image,
    segments,
    latest_image,
    cross_query,
    self_query,
    self_key,
    self_value,
    cross_gate,
    grad_output,
):
    single_float = jnp.float32
    brain_float_half = jnp.bfloat16
    shard_at = lax.axis_index("ctx")
    local_rows = self_query.shape[0]
    head_columns = self_query.shape[1]
    local_heads = cross_gate.shape[0]
    score_scale = 1.0 / math.sqrt(DH)
    slots_here = features.shape[0]
    feat_rows = features.shape[1]
    feat_norm = layer_norm(features.astype(single_float), feat_gain)
    lat_norm = layer_norm(latent_init.astype(single_float), latent_gain)
    res_heads = resamp_query.shape[1] // RESAMPLER_WIDTH
    res_q = jnp.dot(lat_norm, resamp_query, preferred_element_type=single_float).astype(
        brain_float_half
    )
    joined = jnp.concatenate([feat_norm, lat_norm[None]], axis=1)
    res_k = jnp.einsum(
        "sfd,de->sfe", joined, resamp_key, preferred_element_type=single_float
    ).astype(brain_float_half)
    res_v = jnp.einsum(
        "sfd,de->sfe", joined, resamp_value, preferred_element_type=single_float
    ).astype(brain_float_half)
    joined_rows = feat_rows + LATENT_COUNT
    res_score = jnp.einsum(
        "nhe,sfhe->shnf",
        res_q.reshape(LATENT_COUNT, res_heads, RESAMPLER_WIDTH),
        res_k.reshape(slots_here, joined_rows, res_heads, RESAMPLER_WIDTH),
        preferred_element_type=single_float,
    ) / math.sqrt(RESAMPLER_WIDTH)
    res_prob = jax.nn.softmax(res_score, axis=-1).astype(brain_float_half)
    resampler_mixture = jnp.einsum(
        "shnf,sfhe->snhe",
        res_prob,
        res_v.reshape(slots_here, joined_rows, res_heads, RESAMPLER_WIDTH),
        preferred_element_type=single_float,
    ).astype(brain_float_half)
    partial_out = jnp.einsum(
        "uxt,th->uxh",
        resampler_mixture.reshape(slots_here, LATENT_COUNT, res_heads * RESAMPLER_WIDTH),
        resampler_output_weight,
        preferred_element_type=single_float,
    )
    resampled = lax.psum(partial_out, "vis")
    latent_rows = (latent_init.astype(single_float)[None] + resampled).astype(brain_float_half)
    latent_stack = lax.all_gather(latent_rows, "ctx", axis=0, tiled=True)
    cross_key_rows = jnp.einsum(
        "qzv,vc->qzc", latent_stack, cross_key_weight, preferred_element_type=single_float
    ).astype(brain_float_half)
    cross_value_rows = jnp.einsum(
        "qzv,vc->qzc", latent_stack, cross_value_weight, preferred_element_type=single_float
    ).astype(brain_float_half)
    all_slots = cross_key_rows.shape[0]
    key_count = all_slots * LATENT_COUNT
    xkey_rows = cross_key_rows.reshape(key_count, local_heads, DH)
    xvalue_rows = cross_value_rows.reshape(key_count, local_heads, DH)
    col_image = jnp.repeat(slot_image, LATENT_COUNT)
    cquery_rows = cross_query.reshape(local_rows, local_heads, DH)
    cross_allowed = (col_image[None, :] == latest_image[:, None])[None]
    c_prob = masked_softmax(
        jnp.einsum("thd,khd->htk", cquery_rows, xkey_rows, preferred_element_type=single_float)
        * score_scale,
        cross_allowed,
    )
    c_half = c_prob.astype(brain_float_half)
    cross = jnp.einsum("htk,khd->thd", c_half, xvalue_rows, preferred_element_type=single_float)
    gate_tanh = jnp.tanh(cross_gate)[None, :, None]
    value_in = (
        self_value.reshape(local_rows, local_heads, DH).astype(single_float) + gate_tanh * cross
    ).astype(brain_float_half)
    keys_all, values_all = (
        lax.all_gather(self_key, "ctx", axis=0, tiled=True),
        lax.all_gather(value_in.reshape(local_rows, head_columns), "ctx", axis=0, tiled=True),
    )
    total_rows = keys_all.shape[0]
    keys_all = keys_all.reshape(total_rows, local_heads, DH)
    values_all = values_all.reshape(total_rows, local_heads, DH)
    query_rows = self_query.reshape(local_rows, local_heads, DH)
    grad_rows = grad_output.reshape(local_rows, local_heads, DH)
    query_pos = shard_at * local_rows + jnp.arange(local_rows, dtype=jnp.int32)
    key_pos = jnp.arange(total_rows, dtype=jnp.int32)
    query_seg = lax.dynamic_slice_in_dim(segments, shard_at * local_rows, local_rows, 0)
    self_allowed = (
        (query_seg[:, None] == segments[None, :]) & (key_pos[None, :] <= query_pos[:, None])
    )[None]
    self_score = (
        jnp.einsum("thd,khd->htk", query_rows, keys_all, preferred_element_type=single_float)
        * score_scale
    )
    s_prob = masked_softmax(self_score, self_allowed)
    s_half = s_prob.astype(brain_float_half)
    attended = (
        jnp.einsum("htk,khd->thd", s_half, values_all, preferred_element_type=single_float)
        .astype(brain_float_half)
        .reshape(local_rows, head_columns)
    )
    d_prob = jnp.einsum("thd,khd->htk", grad_rows, values_all, preferred_element_type=single_float)
    row_delta = jnp.sum(s_prob * d_prob, axis=-1)
    d_score = (s_prob * (d_prob - row_delta[..., None]) * score_scale).astype(brain_float_half)
    grad_query = (
        jnp.einsum("htk,khd->thd", d_score, keys_all, preferred_element_type=single_float)
        .astype(brain_float_half)
        .reshape(local_rows, head_columns)
    )
    masked_score = jnp.where(self_allowed, self_score, single_float(-1e30))
    row_peak = jnp.max(masked_score, axis=-1)
    row_total = jnp.sum(
        jnp.where(self_allowed, jnp.exp(masked_score - row_peak[..., None]), single_float(0.0)),
        axis=-1,
    )
    log_total = row_peak + jnp.log(row_total)
    query_all, grad_all = (
        lax.all_gather(self_query, "ctx", axis=0, tiled=True),
        lax.all_gather(grad_output, "ctx", axis=0, tiled=True),
    )
    lse_all, delta_all = (
        lax.all_gather(log_total.T, "ctx", axis=0, tiled=True),
        lax.all_gather(row_delta.T, "ctx", axis=0, tiled=True),
    )
    query_all = query_all.reshape(total_rows, local_heads, DH)
    grad_all = grad_all.reshape(total_rows, local_heads, DH)
    own_keys = self_key.reshape(local_rows, local_heads, DH)
    owned_allowed = (
        (segments[:, None] == query_seg[None, :]) & (query_pos[None, :] <= key_pos[:, None])
    )[None]
    back_score = (
        jnp.einsum("qhd,khd->hqk", query_all, own_keys, preferred_element_type=single_float)
        * score_scale
    )
    back_prob = jnp.exp(
        jnp.where(owned_allowed, back_score - lse_all.T[:, :, None], single_float(-1e30))
    )
    back_prob = jnp.where(owned_allowed, back_prob, single_float(0.0))
    back_half = back_prob.astype(brain_float_half)
    back_dprob = jnp.einsum("qhd,khd->hqk", grad_all, value_in, preferred_element_type=single_float)
    back_dscore = (back_prob * (back_dprob - delta_all.T[:, :, None]) * score_scale).astype(
        brain_float_half
    )
    key_sum = jnp.einsum(
        "hqk,qhd->khd", back_dscore, query_all, preferred_element_type=single_float
    ).reshape(local_rows, head_columns)
    vin_sum = jnp.einsum(
        "hqk,qhd->khd", back_half, grad_all, preferred_element_type=single_float
    ).reshape(local_rows, head_columns)
    grad_key = key_sum.astype(brain_float_half)
    grad_value = vin_sum.astype(brain_float_half)
    d_cross = (gate_tanh * vin_sum.reshape(local_rows, local_heads, DH)).astype(brain_float_half)
    c_dprob = jnp.einsum("thd,khd->htk", d_cross, xvalue_rows, preferred_element_type=single_float)
    c_score = (
        c_prob * (c_dprob - jnp.sum(c_prob * c_dprob, axis=-1, keepdims=True)) * score_scale
    ).astype(brain_float_half)
    grad_cross_query = (
        jnp.einsum("htk,khd->thd", c_score, xkey_rows, preferred_element_type=single_float)
        .astype(brain_float_half)
        .reshape(local_rows, head_columns)
    )
    grad_xk = jnp.einsum("htk,thd->khd", c_score, cquery_rows, preferred_element_type=single_float)
    grad_xv = jnp.einsum("htk,thd->khd", c_half, d_cross, preferred_element_type=single_float)
    stacked = jnp.concatenate(
        [
            grad_xk.reshape(all_slots, LATENT_COUNT, head_columns),
            grad_xv.reshape(all_slots, LATENT_COUNT, head_columns),
        ],
        axis=2,
    )
    local_gradients = lax.psum_scatter(stacked, "ctx", scatter_dimension=0, tiled=True).astype(
        brain_float_half
    )
    latent_part = jnp.einsum(
        "zmx,tx->zmt",
        local_gradients[:, :, :head_columns],
        cross_key_weight,
        preferred_element_type=single_float,
    )
    latent_part = latent_part + jnp.einsum(
        "zmx,tx->zmt",
        local_gradients[:, :, head_columns:],
        cross_value_weight,
        preferred_element_type=single_float,
    )
    grad_latents = lax.psum_scatter(latent_part, "vis", scatter_dimension=2, tiled=True).astype(
        brain_float_half
    )
    return (attended, grad_query, grad_key, grad_value, grad_cross_query, grad_latents)


F32 = jnp.float32
BF16 = jnp.bfloat16
MASKED = -1e30


def mm(a, b):
    return lax.dot_general(a, b, (((1,), (0,)), ((), ())), preferred_element_type=F32)


def mm_nt(a, b):
    return lax.dot_general(a, b, (((1,), (1,)), ((), ())), preferred_element_type=F32)


def mm_tn(a, b):
    return lax.dot_general(a, b, (((0,), (0,)), ((), ())), preferred_element_type=F32)


def normed(values, norm_gain):
    v = values.astype(F32)
    center = jnp.mean(v, axis=-1, keepdims=True)
    spread = jnp.mean((v - center) ** 2, axis=-1, keepdims=True)
    return ((v - center) * lax.rsqrt(spread + 1e-05) * norm_gain).astype(BF16)


def head_kernel(
    nc,
    nv,
    feat_in,
    lat0_in,
    fgain_in,
    lgain_in,
    wq_in,
    wk_in,
    wv_in,
    wo_in,
    xwk,
    xwv,
    slot_hbm,
    seg_hbm,
    latest,
    gate_hbm,
    cq_in,
    q_in,
    k_in,
    v_in,
    g_in,
    att_out,
    gq_out,
    gk_out,
    gv_out,
    gcq_out,
    glat_out,
    feat,
    lat0,
    fgain,
    lgain,
    wq,
    wk,
    wv,
    wo,
    slot_in,
    seg_row,
    gate,
    cq,
    q,
    k,
    v,
    g,
    wxk,
    wxv,
    lat_rows,
    lat_col,
    seg_col,
    part,
    part_in,
    lat_mine,
    lat_all,
    xk_loc,
    xv_loc,
    xk,
    xv,
    vin,
    cprob,
    s_buf,
    inv_s,
    o_s,
    dk,
    dv,
    att_s,
    gq_s,
    gk_s,
    gv_s,
    gcq_s,
    gxk,
    gxv,
    gxk_s,
    gxv_s,
    own_k,
    own_v,
    lpart,
    lpart_in,
    w_sem,
    own_sem,
    in_send,
    in_recv,
    lat_send,
    lat_recv,
    p_send,
    p_recv,
    l_send,
    l_recv,
    x_send,
    x_recv,
    o_own,
    o_send,
    o_recv,
    gx_send,
    gx_recv,
    r_send,
    r_recv,
):
    me = lax.axis_index("ctx")
    vi = lax.axis_index("vis")
    rows = q_in.shape[0]
    total = rows * nc
    slots = lat0_in.shape[0]
    wide = lat0_in.shape[1]
    cut = wide // nv
    scale = 1.0 / math.sqrt(DH)
    MESH = pl.DeviceIdType.MESH

    def remote(s, d, ss, rs, c, w):
        return pltpu.make_async_remote_copy(
            src_ref=s, dst_ref=d, send_sem=ss, recv_sem=rs, device_id=(c, w), device_id_type=MESH
        )

    small = (
        (feat_in, feat), (lat0_in, lat0), (fgain_in, fgain), (lgain_in, lgain),
        (wq_in, wq), (wk_in, wk), (wv_in, wv), (wo_in, wo),
        (slot_hbm, slot_in), (seg_hbm, seg_row), (gate_hbm, gate), (latest, lat_rows.at[me]),
    )
    smalls = tuple(
        pltpu.make_async_copy(s, d, w_sem.at[2 + a]) for a, (s, d) in enumerate(small)
    )
    wcopies = (
        pltpu.make_async_copy(xwk, wxk, w_sem.at[0]),
        pltpu.make_async_copy(xwv, wxv, w_sem.at[1]),
    )
    for c in smalls:
        c.start()
    barrier = pltpu.get_barrier_semaphore()
    for o in range(1, nc):
        pl.semaphore_signal(barrier, inc=1, device_id=(lax.rem(me + o, nc), vi), device_id_type=MESH)
    for o in range(1, nv):
        pl.semaphore_signal(barrier, inc=1, device_id=(me, lax.rem(vi + o, nv)), device_id_type=MESH)
    pl.semaphore_wait(barrier, nc + nv - 2)

    def head_of(p):
        return pl.ds(pl.multiple_of(p * DH, DH), DH)

    def rows_of(p):
        return pl.ds(pl.multiple_of(p * rows, rows), rows)

    def slot_of(p):
        return pl.ds(pl.multiple_of(p * slots, slots), slots)

    def cut_of(p):
        return pl.ds(pl.multiple_of(p * cut, cut), cut)

    ins = ((q_in, q), (k_in, k), (cq_in, cq), (v_in, v), (g_in, g))

    def in_copy(a, p):
        return remote(
            ins[a][0].at[:, head_of(p)], ins[a][1].at[rows_of(me), :],
            in_send.at[a, p], in_recv.at[a, me], p, vi,
        )

    def in_wait(a, p):
        return remote(
            ins[a][0].at[:, head_of(p)], ins[a][1].at[rows_of(p), :],
            in_send.at[a, p], in_recv.at[a, p], p, vi,
        )

    def lat_copy(p):
        return remote(latest, lat_rows.at[me], lat_send.at[p], lat_recv.at[me], p, vi)

    def lat_wait(p):
        return remote(latest, lat_rows.at[p], lat_send.at[p], lat_recv.at[p], p, vi)

    def peers(fn):
        def step(o, c):
            fn(lax.rem(me + o, nc))
            return c

        lax.fori_loop(1, nc, step, 0)

    def mates(fn):
        for o in range(1, nv):
            fn(lax.rem(vi + o, nv))

    peers(lambda p: lat_copy(p).start())
    for a in range(5):
        peers(lambda p: in_copy(a, p).start())
    for c in wcopies:
        c.start()
    owns = tuple(
        pltpu.make_async_copy(s.at[:, head_of(me)], d.at[rows_of(me), :], own_sem.at[a])
        for a, (s, d) in enumerate(ins)
    )
    for c in owns:
        c.start()

    for c in smalls:
        c.wait()
    f_norm = normed(feat[0], fgain[...])
    l_norm = normed(lat0[...], lgain[...])
    rq = mm(l_norm, wq[...]).astype(BF16)
    rkf = mm(f_norm, wk[...]).astype(BF16)
    rkl = mm(l_norm, wk[...]).astype(BF16)
    rvf = mm(f_norm, wv[...]).astype(BF16)
    rvl = mm(l_norm, wv[...]).astype(BF16)
    width = rq.shape[1]
    lane = lax.broadcasted_iota(jnp.int32, (1, width), 1)
    mix = jnp.zeros((slots, width), F32)
    r_scale = 1.0 / math.sqrt(RESAMPLER_WIDTH)
    for h in range(width // RESAMPLER_WIDTH):
        inside = (lane >= h * RESAMPLER_WIDTH) & (lane < (h + 1) * RESAMPLER_WIDTH)
        qh = jnp.where(inside, rq, jnp.zeros_like(rq))
        sf = mm_nt(qh, rkf) * r_scale
        sl = mm_nt(qh, rkl) * r_scale
        peak = jnp.maximum(jnp.max(sf, axis=-1, keepdims=True), jnp.max(sl, axis=-1, keepdims=True))
        ef, el = jnp.exp(sf - peak), jnp.exp(sl - peak)
        inv = 1.0 / (jnp.sum(ef, axis=-1, keepdims=True) + jnp.sum(el, axis=-1, keepdims=True))
        mh = mm((ef * inv).astype(BF16), rvf) + mm((el * inv).astype(BF16), rvl)
        mix = jnp.where(inside, mh, mix)
    part[...] = mm(mix.astype(BF16), wo[...])

    def p_copy(w):
        return remote(part.at[:, cut_of(w)], part_in.at[vi], p_send.at[w], p_recv.at[vi], me, w)

    def p_wait(w):
        return remote(part.at[:, cut_of(w)], part_in.at[w], p_send.at[w], p_recv.at[w], me, w)

    mates(lambda w: p_copy(w).start())
    part_in[vi] = part[:, cut_of(vi)]
    mates(lambda w: p_wait(w).wait_recv())
    summed = part_in[0]
    for w in range(1, nv):
        summed = summed + part_in[w]
    lat_mine[...] = (lat0[:, cut_of(vi)].astype(F32) + summed).astype(BF16)

    def l_copy(w):
        return remote(lat_mine, lat_all.at[vi], l_send.at[w], l_recv.at[vi], me, w)

    def l_wait(w):
        return remote(lat_mine, lat_all.at[w], l_send.at[w], l_recv.at[w], me, w)

    mates(lambda w: l_copy(w).start())
    lat_all[vi] = lat_mine[...]
    for c in wcopies:
        c.wait()
    mates(lambda w: l_wait(w).wait_recv())
    for wx, loc in ((wxk, xk_loc), (wxv, xv_loc)):
        acc = mm(lat_all[0], wx[0:cut, :])
        for w in range(1, nv):
            acc = acc + mm(lat_all[w], wx[w * cut : (w + 1) * cut, :])
        loc[...] = acc.astype(BF16)

    xs = ((xk_loc, xk), (xv_loc, xv))

    def x_copy(a, p):
        return remote(
            xs[a][0].at[:, head_of(p)], xs[a][1].at[slot_of(me), :],
            x_send.at[a, p], x_recv.at[a, me], p, vi,
        )

    def x_wait(a, p):
        return remote(
            xs[a][0].at[:, head_of(p)], xs[a][1].at[slot_of(p), :],
            x_send.at[a, p], x_recv.at[a, p], p, vi,
        )

    peers(lambda p: (x_copy(0, p).start(), x_copy(1, p).start()))
    xk[slot_of(me), :] = xk_loc[:, head_of(me)]
    xv[slot_of(me), :] = xv_loc[:, head_of(me)]

    def turned(line):
        return jnp.broadcast_to(line.astype(F32), (128, 128)).T

    for c in range(total // 128):
        seg_col[c * 128 : (c + 1) * 128, :] = turned(seg_row[0:1, c * 128 : (c + 1) * 128])
    kc = 2 * rows

    def key_cols(j):
        return pl.ds(pl.multiple_of(j * kc, kc), kc)

    def wait_in(a):
        owns[a].wait()
        peers(lambda p: in_wait(a, p).wait_recv())

    wait_in(0)
    wait_in(1)

    def lanes(x, op):
        out = x[:, 0:128]
        for c in range(1, kc // 128):
            out = op(out, x[:, c * 128 : (c + 1) * 128])
        return out

    zero = jnp.zeros((rows, 128), F32)

    def soft_step(i, carry):
        r = rows_of(i)
        chunks = i // 2 + 1
        qi = q[r, :]
        seg_i = seg_col[r, 0:1]
        q_pos = i * rows + lax.broadcasted_iota(jnp.int32, (rows, kc), 0)
        k_iota = lax.broadcasted_iota(jnp.int32, (rows, kc), 1)

        def pass1(j, m):
            cols = key_cols(j)
            allowed = (seg_row[0:1, cols].astype(F32) == seg_i) & (j * kc + k_iota <= q_pos)
            s = jnp.where(allowed, mm_nt(qi, k[cols, :]) * scale, MASKED)
            s_buf[r, cols] = s
            return jnp.maximum(m, lanes(s, jnp.maximum))

        m = lax.fori_loop(0, chunks, pass1, jnp.full((rows, 128), MASKED, F32))
        m = jnp.max(m, axis=-1, keepdims=True)

        def pass2(j, tot):
            cols = key_cols(j)
            p = jnp.exp(s_buf[r, cols] - m)
            s_buf[r, cols] = p
            return tot + lanes(p, jnp.add)

        tot = lax.fori_loop(0, chunks, pass2, zero)
        inv_s[r, :] = jnp.broadcast_to(1.0 / jnp.sum(tot, axis=-1, keepdims=True), (rows, 128))
        return carry

    lax.fori_loop(0, nc, soft_step, 0)

    peers(lambda p: lat_wait(p).wait_recv())
    for p in range(nc):
        for c in range(rows // 128):
            lat_col[p * rows + c * 128 : p * rows + (c + 1) * 128, :] = turned(
                lat_rows[p, 0:1, c * 128 : (c + 1) * 128]
            )
    peers(lambda p: (x_wait(0, p).wait_recv(), x_wait(1, p).wait_recv()))
    slot_of_key = lax.broadcasted_iota(jnp.int32, (1, nc * slots), 1) // slots
    images = jnp.zeros((1, nc * slots), F32)
    for p in range(nc):
        images = jnp.where(slot_of_key == p, slot_in[0:1, p : p + 1].astype(F32), images)
    gate_lane = lax.broadcasted_iota(jnp.int32, gate.shape, 1)
    gate_h = jnp.tanh(
        jnp.sum(jnp.where(gate_lane == me, gate[...], 0.0), axis=-1, keepdims=True)
    )
    wait_in(2)
    wait_in(3)

    def cross_step(i, carry):
        r = rows_of(i)
        allowed = images == lat_col[r, 0:1]
        s = jnp.where(allowed, mm_nt(cq[r, :], xk[...]) * scale, MASKED)
        peak = jnp.max(s, axis=-1, keepdims=True)
        e = jnp.where(allowed, jnp.exp(s - peak), 0.0)
        tot = jnp.sum(e, axis=-1, keepdims=True)
        p = e / jnp.where(tot > 0, tot, 1.0)
        cprob[r, :] = p
        crossed = mm(p.astype(BF16), xv[...])
        vin[r, :] = (v[r, :].astype(F32) + gate_h * crossed).astype(BF16)
        return carry

    lax.fori_loop(0, nc, cross_step, 0)

    dk[...] = jnp.zeros_like(dk)
    dv[...] = jnp.zeros_like(dv)
    gxk[...] = jnp.zeros_like(gxk)
    gxv[...] = jnp.zeros_like(gxv)
    outs = ((att_s, att_out), (gq_s, gq_out), (gk_s, gk_out), (gv_s, gv_out), (gcq_s, gcq_out))

    def o_copy(a, p):
        return remote(
            outs[a][0].at[rows_of(p), :], outs[a][1].at[:, head_of(me)],
            o_send.at[a, p], o_recv.at[a, me], p, vi,
        )

    def o_wait(a, p):
        return remote(
            outs[a][0].at[rows_of(p), :], outs[a][1].at[:, head_of(p)],
            o_send.at[a, p], o_recv.at[a, p], p, vi,
        )

    def o_local(a):
        return pltpu.make_async_copy(
            outs[a][0].at[rows_of(me), :], outs[a][1].at[:, head_of(me)], o_own.at[a]
        )

    def send(a, i):
        @pl.when(i != me)
        def _():
            o_copy(a, i).start()

        @pl.when(i == me)
        def _():
            o_local(a).start()

    def att_step(b, carry):
        i = lax.rem(me + 1 + b, nc)
        r = rows_of(i)

        def pass_o(j, acc):
            cols = key_cols(j)
            return acc + mm(s_buf[r, cols].astype(BF16), vin[cols, :])

        o = lax.fori_loop(0, i // 2 + 1, pass_o, zero) * inv_s[r, 0:1]
        o_s[r, :] = o
        att_s[r, :] = o.astype(BF16)
        send(0, i)
        return carry

    lax.fori_loop(0, nc, att_step, 0)
    wait_in(4)

    def self_step(b, carry):
        i = nc - 1 - b
        r = rows_of(i)
        chunks = i // 2 + 1
        qi, gi = q[r, :], g[r, :]
        inv = inv_s[r, 0:1]
        delta = jnp.sum(o_s[r, :] * gi.astype(F32), axis=-1, keepdims=True)

        def pass3(j, acc):
            cols = key_cols(j)
            p = s_buf[r, cols] * inv
            ds = (p * (mm_nt(gi, vin[cols, :]) - delta)).astype(BF16)
            dk[cols, :] += mm_tn(ds, qi)
            dv[cols, :] += mm_tn(p.astype(BF16), gi)
            return acc + mm(ds, k[cols, :])

        gq_s[r, :] = (lax.fori_loop(0, chunks, pass3, zero) * scale).astype(BF16)
        dvi = dv[r, :]
        gk_s[r, :] = (dk[r, :] * scale).astype(BF16)
        gv_s[r, :] = dvi.astype(BF16)

        dc = (gate_h * dvi).astype(BF16)
        cp = cprob[r, :]
        cd = mm_nt(dc, xv[...])
        cs = (cp * (cd - jnp.sum(cp * cd, axis=-1, keepdims=True)) * scale).astype(BF16)
        gcq_s[r, :] = mm(cs, xk[...]).astype(BF16)
        gxk[...] += mm_tn(cs, cq[r, :])
        gxv[...] += mm_tn(cp.astype(BF16), dc)

        send(3, i)
        send(4, i)
        return carry

    lax.fori_loop(0, nc, self_step, 0)

    gxk_s[...] = gxk[...].astype(BF16)
    gxv_s[...] = gxv[...].astype(BF16)
    gxs = ((gxk_s, own_k), (gxv_s, own_v))

    def gx_copy(a, p):
        return remote(
            gxs[a][0].at[slot_of(p), :], gxs[a][1].at[:, head_of(me)],
            gx_send.at[a, p], gx_recv.at[a, me], p, vi,
        )

    def gx_wait(a, p):
        return remote(
            gxs[a][0].at[slot_of(p), :], gxs[a][1].at[:, head_of(p)],
            gx_send.at[a, p], gx_recv.at[a, p], p, vi,
        )

    peers(lambda p: (gx_copy(0, p).start(), gx_copy(1, p).start()))
    send_o = lambda a: (o_local(a).start(), peers(lambda p: o_copy(a, p).start()))
    send_o(1)
    send_o(2)
    own_k[:, head_of(me)] = gxk_s[slot_of(me), :]
    own_v[:, head_of(me)] = gxv_s[slot_of(me), :]
    peers(lambda p: (gx_wait(0, p).wait_recv(), gx_wait(1, p).wait_recv()))
    lpart[...] = mm_nt(own_k[...], wxk[...]) + mm_nt(own_v[...], wxv[...])

    def r_copy(w):
        return remote(lpart.at[:, cut_of(w)], lpart_in.at[vi], r_send.at[w], r_recv.at[vi], me, w)

    def r_wait(w):
        return remote(lpart.at[:, cut_of(w)], lpart_in.at[w], r_send.at[w], r_recv.at[w], me, w)

    mates(lambda w: r_copy(w).start())
    lpart_in[vi] = lpart[:, cut_of(vi)]
    mates(lambda w: r_wait(w).wait_recv())
    summed = lpart_in[0]
    for w in range(1, nv):
        summed = summed + lpart_in[w]
    glat_out[0] = summed.astype(BF16)

    def finish(p):
        lat_wait(p).wait_send()
        for a in range(5):
            in_wait(a, p).wait_send()
            o_wait(a, p).wait()
        for a in range(2):
            x_wait(a, p).wait_send()
            gx_wait(a, p).wait_send()

    peers(finish)

    def finish_mate(w):
        p_wait(w).wait_send()
        l_wait(w).wait_send()
        r_wait(w).wait_send()

    mates(finish_mate)
    for a in range(5):
        o_local(a).wait()


def by_head(nc, nv, *args):
    (feat, lat0, fgain, lgain, wq, wk, wv, wo, xwk, xwv, slot_image, segments, latest_image,
     cross_query, self_query, self_key, self_value, cross_gate, grad_output) = args
    rows, cols = self_query.shape
    total = rows * nc
    slots, wide = lat0.shape
    xrows = nc * slots
    cut = wide // nv
    vmem = pl.BlockSpec(memory_space=pltpu.VMEM)
    hbm = pl.BlockSpec(memory_space=pltpu.HBM)
    tok = jax.ShapeDtypeStruct((rows, cols), BF16)
    V = pltpu.VMEM
    dma = pltpu.SemaphoreType.DMA
    scratch = (
        [V((1,) + feat.shape[1:], BF16), V((slots, wide), BF16)]
        + [V((1, wide), F32)] * 2
        + [V(wq.shape, BF16)] * 3
        + [V(wo.shape, BF16)]
        + [V((1, nc), jnp.int32), V((1, total), jnp.int32), V((1, nc), F32)]
        + [V((total, DH), BF16)] * 5
        + [V((wide, cols), BF16)] * 2
        + [V((nc, 1, rows), jnp.int32)] + [V((total, 128), F32)] * 2
        + [V((slots, wide), F32), V((nv, slots, cut), F32)]
        + [V((slots, cut), BF16), V((nv, slots, cut), BF16)]
        + [V((slots, cols), BF16)] * 2
        + [V((xrows, DH), BF16)] * 2
        + [V((total, DH), BF16), V((total, xrows), F32)]
        + [V((total, total), F32)] + [V((total, DH), F32)] * 2
        + [V((total, DH), F32)] * 2
        + [V((total, DH), BF16)] * 5
        + [V((xrows, DH), F32)] * 2
        + [V((xrows, DH), BF16)] * 2
        + [V((slots, cols), BF16)] * 2
        + [V((slots, wide), F32), V((nv, slots, cut), F32)]
        + [dma((14,)), dma((5,))]
        + [dma((5, nc))] * 2
        + [dma((nc,))] * 2
        + [dma((nv,))] * 4
        + [dma((2, nc))] * 2
        + [dma((5,))]
        + [dma((5, nc))] * 2
        + [dma((2, nc))] * 2
        + [dma((nv,))] * 2
    )
    got = pl.pallas_call(
        functools.partial(head_kernel, nc, nv),
        out_shape=[tok] * 5 + [jax.ShapeDtypeStruct((1, slots, cut), BF16)],
        in_specs=[hbm] * 19,
        out_specs=[hbm] * 5 + [vmem],
        scratch_shapes=scratch,
        compiler_params=pltpu.CompilerParams(
            collective_id=0, has_side_effects=True, vmem_limit_bytes=62 * 1024 * 1024
        ),
        name="head_window",
    )(feat, lat0, fgain[None], lgain[None], wq, wk, wv, wo, xwk, xwv, slot_image[None],
      segments[None], latest_image[None], cross_gate[None], cross_query, self_query, self_key,
      self_value, grad_output)
    moved = pl.pallas_call(
        copy_kernel,
        out_shape=[tok] * 5,
        in_specs=[hbm] * 5,
        out_specs=[hbm] * 5,
        scratch_shapes=[V(tok.shape, BF16)] * 5 + [dma((2, 5))],
        name="results",
    )(*got[:5])
    return (*moved, got[5])


def copy_kernel(*refs):
    src, dst, held, sem = refs[:5], refs[5:10], refs[10:15], refs[15]
    first = [pltpu.make_async_copy(src[a], held[a], sem.at[0, a]) for a in range(5)]
    second = [pltpu.make_async_copy(held[a], dst[a], sem.at[1, a]) for a in range(5)]
    for c in first:
        c.start()
    for a in range(5):
        first[a].wait()
        second[a].start()
    for c in second:
        c.wait()


def dispatch(nc, nv, *args):
    if args[17].shape[0] == nc and args[0].shape[0] == 1:
        return tuple(by_head(nc, nv, *args))
    return shards(*args)


def solution(mesh):
    in_specs = (
        P("ctx", None, None),
        P(),
        P(),
        P(),
        P(None, "vis"),
        P(None, "vis"),
        P(None, "vis"),
        P("vis", None),
        P(None, "vis"),
        P(None, "vis"),
        P(),
        P(),
        P("ctx"),
        P("ctx", "vis"),
        P("ctx", "vis"),
        P("ctx", "vis"),
        P("ctx", "vis"),
        P("vis"),
        P("ctx", "vis"),
    )
    out_specs = (
        P("ctx", "vis"),
        P("ctx", "vis"),
        P("ctx", "vis"),
        P("ctx", "vis"),
        P("ctx", "vis"),
        P("ctx", None, "vis"),
    )
    body = functools.partial(dispatch, mesh.shape["ctx"], mesh.shape["vis"])
    return jax.shard_map(body, mesh=mesh, in_specs=in_specs, out_specs=out_specs, check_vma=False)
```

```python
import functools
import math

import jax
import jax.numpy as jnp
from jax import lax
from jax.experimental import pallas as pl
from jax.experimental.pallas import tpu as pltpu
from jax.sharding import PartitionSpec as P

LATENT_COUNT = 64
RESAMPLER_WIDTH = 64
DH = 128


def layer_norm(values, norm_gain):
    center = jnp.mean(values, axis=-1, keepdims=True)
    spread = jnp.mean((values - center) ** 2, axis=-1, keepdims=True)
    return ((values - center) * lax.rsqrt(spread + 1e-05) * norm_gain).astype(jnp.bfloat16)


def masked_softmax(scores, allowed):
    masked = jnp.where(allowed, scores, jnp.float32(-1e30))
    peak = jnp.max(masked, axis=-1, keepdims=True)
    raised = jnp.where(allowed, jnp.exp(masked - peak), jnp.float32(0.0))
    summed = jnp.sum(raised, axis=-1, keepdims=True)
    return raised / jnp.where(summed > 0, summed, jnp.float32(1.0))


def shards(
    features,
    latent_init,
    feat_gain,
    latent_gain,
    resamp_query,
    resamp_key,
    resamp_value,
    resampler_output_weight,
    cross_key_weight,
    cross_value_weight,
    slot_image,
    segments,
    latest_image,
    cross_query,
    self_query,
    self_key,
    self_value,
    cross_gate,
    grad_output,
):
    single_float = jnp.float32
    brain_float_half = jnp.bfloat16
    shard_at = lax.axis_index("ctx")
    local_rows = self_query.shape[0]
    head_columns = self_query.shape[1]
    local_heads = cross_gate.shape[0]
    score_scale = 1.0 / math.sqrt(DH)
    slots_here = features.shape[0]
    feat_rows = features.shape[1]
    feat_norm = layer_norm(features.astype(single_float), feat_gain)
    lat_norm = layer_norm(latent_init.astype(single_float), latent_gain)
    res_heads = resamp_query.shape[1] // RESAMPLER_WIDTH
    res_q = jnp.dot(lat_norm, resamp_query, preferred_element_type=single_float).astype(
        brain_float_half
    )
    joined = jnp.concatenate([feat_norm, lat_norm[None]], axis=1)
    res_k = jnp.einsum(
        "sfd,de->sfe", joined, resamp_key, preferred_element_type=single_float
    ).astype(brain_float_half)
    res_v = jnp.einsum(
        "sfd,de->sfe", joined, resamp_value, preferred_element_type=single_float
    ).astype(brain_float_half)
    joined_rows = feat_rows + LATENT_COUNT
    res_score = jnp.einsum(
        "nhe,sfhe->shnf",
        res_q.reshape(LATENT_COUNT, res_heads, RESAMPLER_WIDTH),
        res_k.reshape(slots_here, joined_rows, res_heads, RESAMPLER_WIDTH),
        preferred_element_type=single_float,
    ) / math.sqrt(RESAMPLER_WIDTH)
    res_prob = jax.nn.softmax(res_score, axis=-1).astype(brain_float_half)
    resampler_mixture = jnp.einsum(
        "shnf,sfhe->snhe",
        res_prob,
        res_v.reshape(slots_here, joined_rows, res_heads, RESAMPLER_WIDTH),
        preferred_element_type=single_float,
    ).astype(brain_float_half)
    partial_out = jnp.einsum(
        "uxt,th->uxh",
        resampler_mixture.reshape(slots_here, LATENT_COUNT, res_heads * RESAMPLER_WIDTH),
        resampler_output_weight,
        preferred_element_type=single_float,
    )
    resampled = lax.psum(partial_out, "vis")
    latent_rows = (latent_init.astype(single_float)[None] + resampled).astype(brain_float_half)
    latent_stack = lax.all_gather(latent_rows, "ctx", axis=0, tiled=True)
    cross_key_rows = jnp.einsum(
        "qzv,vc->qzc", latent_stack, cross_key_weight, preferred_element_type=single_float
    ).astype(brain_float_half)
    cross_value_rows = jnp.einsum(
        "qzv,vc->qzc", latent_stack, cross_value_weight, preferred_element_type=single_float
    ).astype(brain_float_half)
    all_slots = cross_key_rows.shape[0]
    key_count = all_slots * LATENT_COUNT
    xkey_rows = cross_key_rows.reshape(key_count, local_heads, DH)
    xvalue_rows = cross_value_rows.reshape(key_count, local_heads, DH)
    col_image = jnp.repeat(slot_image, LATENT_COUNT)
    cquery_rows = cross_query.reshape(local_rows, local_heads, DH)
    cross_allowed = (col_image[None, :] == latest_image[:, None])[None]
    c_prob = masked_softmax(
        jnp.einsum("thd,khd->htk", cquery_rows, xkey_rows, preferred_element_type=single_float)
        * score_scale,
        cross_allowed,
    )
    c_half = c_prob.astype(brain_float_half)
    cross = jnp.einsum("htk,khd->thd", c_half, xvalue_rows, preferred_element_type=single_float)
    gate_tanh = jnp.tanh(cross_gate)[None, :, None]
    value_in = (
        self_value.reshape(local_rows, local_heads, DH).astype(single_float) + gate_tanh * cross
    ).astype(brain_float_half)
    keys_all, values_all = (
        lax.all_gather(self_key, "ctx", axis=0, tiled=True),
        lax.all_gather(value_in.reshape(local_rows, head_columns), "ctx", axis=0, tiled=True),
    )
    total_rows = keys_all.shape[0]
    keys_all = keys_all.reshape(total_rows, local_heads, DH)
    values_all = values_all.reshape(total_rows, local_heads, DH)
    query_rows = self_query.reshape(local_rows, local_heads, DH)
    grad_rows = grad_output.reshape(local_rows, local_heads, DH)
    query_pos = shard_at * local_rows + jnp.arange(local_rows, dtype=jnp.int32)
    key_pos = jnp.arange(total_rows, dtype=jnp.int32)
    query_seg = lax.dynamic_slice_in_dim(segments, shard_at * local_rows, local_rows, 0)
    self_allowed = (
        (query_seg[:, None] == segments[None, :]) & (key_pos[None, :] <= query_pos[:, None])
    )[None]
    self_score = (
        jnp.einsum("thd,khd->htk", query_rows, keys_all, preferred_element_type=single_float)
        * score_scale
    )
    s_prob = masked_softmax(self_score, self_allowed)
    s_half = s_prob.astype(brain_float_half)
    attended = (
        jnp.einsum("htk,khd->thd", s_half, values_all, preferred_element_type=single_float)
        .astype(brain_float_half)
        .reshape(local_rows, head_columns)
    )
    d_prob = jnp.einsum("thd,khd->htk", grad_rows, values_all, preferred_element_type=single_float)
    row_delta = jnp.sum(s_prob * d_prob, axis=-1)
    d_score = (s_prob * (d_prob - row_delta[..., None]) * score_scale).astype(brain_float_half)
    grad_query = (
        jnp.einsum("htk,khd->thd", d_score, keys_all, preferred_element_type=single_float)
        .astype(brain_float_half)
        .reshape(local_rows, head_columns)
    )
    masked_score = jnp.where(self_allowed, self_score, single_float(-1e30))
    row_peak = jnp.max(masked_score, axis=-1)
    row_total = jnp.sum(
        jnp.where(self_allowed, jnp.exp(masked_score - row_peak[..., None]), single_float(0.0)),
        axis=-1,
    )
    log_total = row_peak + jnp.log(row_total)
    query_all, grad_all = (
        lax.all_gather(self_query, "ctx", axis=0, tiled=True),
        lax.all_gather(grad_output, "ctx", axis=0, tiled=True),
    )
    lse_all, delta_all = (
        lax.all_gather(log_total.T, "ctx", axis=0, tiled=True),
        lax.all_gather(row_delta.T, "ctx", axis=0, tiled=True),
    )
    query_all = query_all.reshape(total_rows, local_heads, DH)
    grad_all = grad_all.reshape(total_rows, local_heads, DH)
    own_keys = self_key.reshape(local_rows, local_heads, DH)
    owned_allowed = (
        (segments[:, None] == query_seg[None, :]) & (query_pos[None, :] <= key_pos[:, None])
    )[None]
    back_score = (
        jnp.einsum("qhd,khd->hqk", query_all, own_keys, preferred_element_type=single_float)
        * score_scale
    )
    back_prob = jnp.exp(
        jnp.where(owned_allowed, back_score - lse_all.T[:, :, None], single_float(-1e30))
    )
    back_prob = jnp.where(owned_allowed, back_prob, single_float(0.0))
    back_half = back_prob.astype(brain_float_half)
    back_dprob = jnp.einsum("qhd,khd->hqk", grad_all, value_in, preferred_element_type=single_float)
    back_dscore = (back_prob * (back_dprob - delta_all.T[:, :, None]) * score_scale).astype(
        brain_float_half
    )
    key_sum = jnp.einsum(
        "hqk,qhd->khd", back_dscore, query_all, preferred_element_type=single_float
    ).reshape(local_rows, head_columns)
    vin_sum = jnp.einsum(
        "hqk,qhd->khd", back_half, grad_all, preferred_element_type=single_float
    ).reshape(local_rows, head_columns)
    grad_key = key_sum.astype(brain_float_half)
    grad_value = vin_sum.astype(brain_float_half)
    d_cross = (gate_tanh * vin_sum.reshape(local_rows, local_heads, DH)).astype(brain_float_half)
    c_dprob = jnp.einsum("thd,khd->htk", d_cross, xvalue_rows, preferred_element_type=single_float)
    c_score = (
        c_prob * (c_dprob - jnp.sum(c_prob * c_dprob, axis=-1, keepdims=True)) * score_scale
    ).astype(brain_float_half)
    grad_cross_query = (
        jnp.einsum("htk,khd->thd", c_score, xkey_rows, preferred_element_type=single_float)
        .astype(brain_float_half)
        .reshape(local_rows, head_columns)
    )
    grad_xk = jnp.einsum("htk,thd->khd", c_score, cquery_rows, preferred_element_type=single_float)
    grad_xv = jnp.einsum("htk,thd->khd", c_half, d_cross, preferred_element_type=single_float)
    stacked = jnp.concatenate(
        [
            grad_xk.reshape(all_slots, LATENT_COUNT, head_columns),
            grad_xv.reshape(all_slots, LATENT_COUNT, head_columns),
        ],
        axis=2,
    )
    local_gradients = lax.psum_scatter(stacked, "ctx", scatter_dimension=0, tiled=True).astype(
        brain_float_half
    )
    latent_part = jnp.einsum(
        "zmx,tx->zmt",
        local_gradients[:, :, :head_columns],
        cross_key_weight,
        preferred_element_type=single_float,
    )
    latent_part = latent_part + jnp.einsum(
        "zmx,tx->zmt",
        local_gradients[:, :, head_columns:],
        cross_value_weight,
        preferred_element_type=single_float,
    )
    grad_latents = lax.psum_scatter(latent_part, "vis", scatter_dimension=2, tiled=True).astype(
        brain_float_half
    )
    return (attended, grad_query, grad_key, grad_value, grad_cross_query, grad_latents)


F32 = jnp.float32
BF16 = jnp.bfloat16
MASKED = -1e30


def mm(a, b):
    return lax.dot_general(a, b, (((1,), (0,)), ((), ())), preferred_element_type=F32)


def mm_nt(a, b):
    return lax.dot_general(a, b, (((1,), (1,)), ((), ())), preferred_element_type=F32)


def mm_tn(a, b):
    return lax.dot_general(a, b, (((0,), (0,)), ((), ())), preferred_element_type=F32)


def normed(values, norm_gain):
    v = values.astype(F32)
    center = jnp.mean(v, axis=-1, keepdims=True)
    spread = jnp.mean((v - center) ** 2, axis=-1, keepdims=True)
    return ((v - center) * lax.rsqrt(spread + 1e-05) * norm_gain).astype(BF16)


def head_kernel(
    nc,
    nv,
    feat_in,
    lat0_in,
    fgain_in,
    lgain_in,
    wq_in,
    wk_in,
    wv_in,
    wo_in,
    xwk,
    xwv,
    slot_hbm,
    seg_hbm,
    latest,
    gate_hbm,
    cq_in,
    q_in,
    k_in,
    v_in,
    g_in,
    att_out,
    gq_out,
    gk_out,
    gv_out,
    gcq_out,
    glat_out,
    feat,
    lat0,
    fgain,
    lgain,
    wq,
    wk,
    wv,
    wo,
    slot_in,
    seg_row,
    gate,
    cq,
    q,
    k,
    v,
    g,
    wxk,
    wxv,
    lat_rows,
    lat_col,
    seg_col,
    part,
    part_in,
    lat_mine,
    lat_all,
    xk_loc,
    xv_loc,
    xk,
    xv,
    vin,
    cprob,
    s_buf,
    inv_s,
    o_s,
    dk,
    dv,
    att_s,
    gq_s,
    gk_s,
    gv_s,
    gcq_s,
    gxk,
    gxv,
    gxk_s,
    gxv_s,
    own_k,
    own_v,
    lpart,
    lpart_in,
    w_sem,
    own_sem,
    in_send,
    in_recv,
    lat_send,
    lat_recv,
    p_send,
    p_recv,
    l_send,
    l_recv,
    x_send,
    x_recv,
    o_own,
    o_send,
    o_recv,
    gx_send,
    gx_recv,
    r_send,
    r_recv,
):
    me = lax.axis_index("ctx")
    vi = lax.axis_index("vis")
    rows = q_in.shape[0]
    total = rows * nc
    slots = lat0_in.shape[0]
    wide = lat0_in.shape[1]
    cut = wide // nv
    scale = 1.0 / math.sqrt(DH)
    MESH = pl.DeviceIdType.MESH

    def remote(s, d, ss, rs, c, w):
        return pltpu.make_async_remote_copy(
            src_ref=s, dst_ref=d, send_sem=ss, recv_sem=rs, device_id=(c, w), device_id_type=MESH
        )

    small = (
        (feat_in, feat), (lat0_in, lat0), (fgain_in, fgain), (lgain_in, lgain),
        (wq_in, wq), (wk_in, wk), (wv_in, wv), (wo_in, wo),
        (slot_hbm, slot_in), (seg_hbm, seg_row), (gate_hbm, gate), (latest, lat_rows.at[me]),
    )
    smalls = tuple(
        pltpu.make_async_copy(s, d, w_sem.at[2 + a]) for a, (s, d) in enumerate(small)
    )
    wcopies = (
        pltpu.make_async_copy(xwk, wxk, w_sem.at[0]),
        pltpu.make_async_copy(xwv, wxv, w_sem.at[1]),
    )
    for c in smalls:
        c.start()
    barrier = pltpu.get_barrier_semaphore()
    for o in range(1, nc):
        pl.semaphore_signal(barrier, inc=1, device_id=(lax.rem(me + o, nc), vi), device_id_type=MESH)
    for o in range(1, nv):
        pl.semaphore_signal(barrier, inc=1, device_id=(me, lax.rem(vi + o, nv)), device_id_type=MESH)
    pl.semaphore_wait(barrier, nc + nv - 2)

    def head_of(p):
        return pl.ds(pl.multiple_of(p * DH, DH), DH)

    def rows_of(p):
        return pl.ds(pl.multiple_of(p * rows, rows), rows)

    def slot_of(p):
        return pl.ds(pl.multiple_of(p * slots, slots), slots)

    def cut_of(p):
        return pl.ds(pl.multiple_of(p * cut, cut), cut)

    ins = ((q_in, q), (k_in, k), (cq_in, cq), (v_in, v), (g_in, g))

    def in_copy(a, p):
        return remote(
            ins[a][0].at[:, head_of(p)], ins[a][1].at[rows_of(me), :],
            in_send.at[a, p], in_recv.at[a, me], p, vi,
        )

    def in_wait(a, p):
        return remote(
            ins[a][0].at[:, head_of(p)], ins[a][1].at[rows_of(p), :],
            in_send.at[a, p], in_recv.at[a, p], p, vi,
        )

    def lat_copy(p):
        return remote(latest, lat_rows.at[me], lat_send.at[p], lat_recv.at[me], p, vi)

    def lat_wait(p):
        return remote(latest, lat_rows.at[p], lat_send.at[p], lat_recv.at[p], p, vi)

    def peers(fn):
        def step(o, c):
            fn(lax.rem(me + o, nc))
            return c

        lax.fori_loop(1, nc, step, 0)

    def mates(fn):
        for o in range(1, nv):
            fn(lax.rem(vi + o, nv))

    peers(lambda p: lat_copy(p).start())
    for a in range(2):
        peers(lambda p: in_copy(a, p).start())
    for c in wcopies:
        c.start()
    owns = tuple(
        pltpu.make_async_copy(s.at[:, head_of(me)], d.at[rows_of(me), :], own_sem.at[a])
        for a, (s, d) in enumerate(ins)
    )
    for c in owns:
        c.start()

    for c in smalls:
        c.wait()
    def flat(gain):
        return jnp.concatenate([gain[c : c + 1, :] for c in range(wide // 128)], axis=1)

    f_norm = normed(feat[0], flat(fgain))
    l_norm = normed(lat0[...], flat(lgain))
    rq = mm(l_norm, wq[...]).astype(BF16)
    rkf = mm(f_norm, wk[...]).astype(BF16)
    rkl = mm(l_norm, wk[...]).astype(BF16)
    rvf = mm(f_norm, wv[...]).astype(BF16)
    rvl = mm(l_norm, wv[...]).astype(BF16)
    width = rq.shape[1]
    lane = lax.broadcasted_iota(jnp.int32, (1, width), 1)
    mix = jnp.zeros((slots, width), F32)
    r_scale = 1.0 / math.sqrt(RESAMPLER_WIDTH)
    for h in range(width // RESAMPLER_WIDTH):
        inside = (lane >= h * RESAMPLER_WIDTH) & (lane < (h + 1) * RESAMPLER_WIDTH)
        qh = jnp.where(inside, rq, jnp.zeros_like(rq))
        sf = mm_nt(qh, rkf) * r_scale
        sl = mm_nt(qh, rkl) * r_scale
        peak = jnp.maximum(jnp.max(sf, axis=-1, keepdims=True), jnp.max(sl, axis=-1, keepdims=True))
        ef, el = jnp.exp(sf - peak), jnp.exp(sl - peak)
        inv = 1.0 / (jnp.sum(ef, axis=-1, keepdims=True) + jnp.sum(el, axis=-1, keepdims=True))
        mh = mm((ef * inv).astype(BF16), rvf) + mm((el * inv).astype(BF16), rvl)
        mix = jnp.where(inside, mh, mix)
    part[...] = mm(mix.astype(BF16), wo[...])

    def p_copy(w):
        return remote(part.at[:, cut_of(w)], part_in.at[vi], p_send.at[w], p_recv.at[vi], me, w)

    def p_wait(w):
        return remote(part.at[:, cut_of(w)], part_in.at[w], p_send.at[w], p_recv.at[w], me, w)

    mates(lambda w: p_copy(w).start())
    part_in[vi] = part[:, cut_of(vi)]
    mates(lambda w: p_wait(w).wait_recv())
    summed = part_in[0]
    for w in range(1, nv):
        summed = summed + part_in[w]
    lat_mine[...] = (lat0[:, cut_of(vi)].astype(F32) + summed).astype(BF16)

    def l_copy(w):
        return remote(lat_mine, lat_all.at[vi], l_send.at[w], l_recv.at[vi], me, w)

    def l_wait(w):
        return remote(lat_mine, lat_all.at[w], l_send.at[w], l_recv.at[w], me, w)

    mates(lambda w: l_copy(w).start())
    lat_all[vi] = lat_mine[...]
    for c in wcopies:
        c.wait()
    mates(lambda w: l_wait(w).wait_recv())
    for wx, loc in ((wxk, xk_loc), (wxv, xv_loc)):
        acc = mm(lat_all[0], wx[0:cut, :])
        for w in range(1, nv):
            acc = acc + mm(lat_all[w], wx[w * cut : (w + 1) * cut, :])
        loc[...] = acc.astype(BF16)

    xs = ((xk_loc, xk), (xv_loc, xv))

    def x_copy(a, p):
        return remote(
            xs[a][0].at[:, head_of(p)], xs[a][1].at[slot_of(me), :],
            x_send.at[a, p], x_recv.at[a, me], p, vi,
        )

    def x_wait(a, p):
        return remote(
            xs[a][0].at[:, head_of(p)], xs[a][1].at[slot_of(p), :],
            x_send.at[a, p], x_recv.at[a, p], p, vi,
        )

    peers(lambda p: (x_copy(0, p).start(), x_copy(1, p).start()))
    for a in range(2, 5):
        peers(lambda p: in_copy(a, p).start())
    xk[slot_of(me), :] = xk_loc[:, head_of(me)]
    xv[slot_of(me), :] = xv_loc[:, head_of(me)]

    def turned(line):
        return jnp.broadcast_to(line.astype(F32), (128, 128)).T

    for c in range(total // 128):
        seg_col[c * 128 : (c + 1) * 128, :] = turned(seg_row[0:1, c * 128 : (c + 1) * 128])
    kc = 2 * rows

    def key_cols(j):
        return pl.ds(pl.multiple_of(j * kc, kc), kc)

    def wait_in(a):
        owns[a].wait()
        peers(lambda p: in_wait(a, p).wait_recv())

    wait_in(0)
    wait_in(1)

    def lanes(x, op):
        out = x[:, 0:128]
        for c in range(1, kc // 128):
            out = op(out, x[:, c * 128 : (c + 1) * 128])
        return out

    zero = jnp.zeros((rows, 128), F32)

    def soft_step(i, carry):
        r = rows_of(i)
        chunks = i // 2 + 1
        qi = q[r, :]
        seg_i = seg_col[r, 0:1]
        q_pos = i * rows + lax.broadcasted_iota(jnp.int32, (rows, kc), 0)
        k_iota = lax.broadcasted_iota(jnp.int32, (rows, kc), 1)

        def pass1(j, m):
            cols = key_cols(j)
            allowed = (seg_row[0:1, cols].astype(F32) == seg_i) & (j * kc + k_iota <= q_pos)
            s = jnp.where(allowed, mm_nt(qi, k[cols, :]) * scale, MASKED)
            s_buf[r, cols] = s
            return jnp.maximum(m, lanes(s, jnp.maximum))

        m = lax.fori_loop(0, chunks, pass1, jnp.full((rows, 128), MASKED, F32))
        m = jnp.max(m, axis=-1, keepdims=True)

        def pass2(j, tot):
            cols = key_cols(j)
            p = jnp.exp(s_buf[r, cols] - m)
            s_buf[r, cols] = p
            return tot + lanes(p, jnp.add)

        tot = lax.fori_loop(0, chunks, pass2, zero)
        inv_s[r, :] = jnp.broadcast_to(1.0 / jnp.sum(tot, axis=-1, keepdims=True), (rows, 128))
        return carry

    lax.fori_loop(0, nc, soft_step, 0)

    peers(lambda p: lat_wait(p).wait_recv())
    for p in range(nc):
        for c in range(rows // 128):
            lat_col[p * rows + c * 128 : p * rows + (c + 1) * 128, :] = turned(
                lat_rows[p, 0:1, c * 128 : (c + 1) * 128]
            )
    peers(lambda p: (x_wait(0, p).wait_recv(), x_wait(1, p).wait_recv()))
    slot_of_key = lax.broadcasted_iota(jnp.int32, (1, nc * slots), 1) // slots
    images = jnp.zeros((1, nc * slots), F32)
    for p in range(nc):
        images = jnp.where(slot_of_key == p, slot_in[0:1, p : p + 1].astype(F32), images)
    gate_lane = lax.broadcasted_iota(jnp.int32, gate.shape, 1)
    gate_h = jnp.tanh(
        jnp.sum(jnp.where(gate_lane == me, gate[...], 0.0), axis=-1, keepdims=True)
    )
    wait_in(2)
    wait_in(3)

    def cross_step(i, carry):
        r = rows_of(i)
        allowed = images == lat_col[r, 0:1]
        s = jnp.where(allowed, mm_nt(cq[r, :], xk[...]) * scale, MASKED)
        peak = jnp.max(s, axis=-1, keepdims=True)
        e = jnp.where(allowed, jnp.exp(s - peak), 0.0)
        tot = jnp.sum(e, axis=-1, keepdims=True)
        p = e / jnp.where(tot > 0, tot, 1.0)
        cprob[r, :] = p
        crossed = mm(p.astype(BF16), xv[...])
        vin[r, :] = (v[r, :].astype(F32) + gate_h * crossed).astype(BF16)
        return carry

    lax.fori_loop(0, nc, cross_step, 0)

    dk[...] = jnp.zeros_like(dk)
    dv[...] = jnp.zeros_like(dv)
    gxk[...] = jnp.zeros_like(gxk)
    gxv[...] = jnp.zeros_like(gxv)
    outs = ((att_s, att_out), (gq_s, gq_out), (gk_s, gk_out), (gv_s, gv_out), (gcq_s, gcq_out))

    def o_copy(a, p):
        return remote(
            outs[a][0].at[rows_of(p), :], outs[a][1].at[:, head_of(me)],
            o_send.at[a, p], o_recv.at[a, me], p, vi,
        )

    def o_wait(a, p):
        return remote(
            outs[a][0].at[rows_of(p), :], outs[a][1].at[:, head_of(p)],
            o_send.at[a, p], o_recv.at[a, p], p, vi,
        )

    def o_local(a):
        return pltpu.make_async_copy(
            outs[a][0].at[rows_of(me), :], outs[a][1].at[:, head_of(me)], o_own.at[a]
        )

    def send(a, i):
        @pl.when(i != me)
        def _():
            o_copy(a, i).start()

        @pl.when(i == me)
        def _():
            o_local(a).start()

    def att_step(b, carry):
        i = lax.rem(me + 1 + b, nc)
        r = rows_of(i)

        def pass_o(j, acc):
            cols = key_cols(j)
            return acc + mm(s_buf[r, cols].astype(BF16), vin[cols, :])

        o = lax.fori_loop(0, i // 2 + 1, pass_o, zero) * inv_s[r, 0:1]
        o_s[r, :] = o
        att_s[r, :] = o.astype(BF16)
        send(0, i)
        return carry

    lax.fori_loop(0, nc, att_step, 0)
    wait_in(4)

    def self_step(b, carry):
        i = lax.rem(me + 1 + b, nc)
        r = rows_of(i)
        chunks = i // 2 + 1
        qi, gi = q[r, :], g[r, :]
        inv = inv_s[r, 0:1]
        delta = jnp.sum(o_s[r, :] * gi.astype(F32), axis=-1, keepdims=True)

        def pass3(j, acc):
            cols = key_cols(j)
            p = s_buf[r, cols] * inv
            ds = (p * (mm_nt(gi, vin[cols, :]) - delta)).astype(BF16)
            dk[cols, :] += mm_tn(ds, qi)
            dv[cols, :] += mm_tn(p.astype(BF16), gi)
            return acc + mm(ds, k[cols, :])

        gq_s[r, :] = (lax.fori_loop(0, chunks, pass3, zero) * scale).astype(BF16)
        send(1, i)
        return carry

    lax.fori_loop(0, nc, self_step, 0)

    def back_step(b, carry):
        i = lax.rem(me + 1 + b, nc)
        r = rows_of(i)
        dvi = dv[r, :]
        gk_s[r, :] = (dk[r, :] * scale).astype(BF16)
        gv_s[r, :] = dvi.astype(BF16)

        dc = (gate_h * dvi).astype(BF16)
        cp = cprob[r, :]
        cd = mm_nt(dc, xv[...])
        cs = (cp * (cd - jnp.sum(cp * cd, axis=-1, keepdims=True)) * scale).astype(BF16)
        gcq_s[r, :] = mm(cs, xk[...]).astype(BF16)
        gxk[...] += mm_tn(cs, cq[r, :])
        gxv[...] += mm_tn(cp.astype(BF16), dc)

        send(3, i)
        send(4, i)
        return carry

    lax.fori_loop(0, nc, back_step, 0)

    gxk_s[...] = gxk[...].astype(BF16)
    gxv_s[...] = gxv[...].astype(BF16)
    gxs = ((gxk_s, own_k), (gxv_s, own_v))

    def gx_copy(a, p):
        return remote(
            gxs[a][0].at[slot_of(p), :], gxs[a][1].at[:, head_of(me)],
            gx_send.at[a, p], gx_recv.at[a, me], p, vi,
        )

    def gx_wait(a, p):
        return remote(
            gxs[a][0].at[slot_of(p), :], gxs[a][1].at[:, head_of(p)],
            gx_send.at[a, p], gx_recv.at[a, p], p, vi,
        )

    peers(lambda p: (gx_copy(0, p).start(), gx_copy(1, p).start()))
    send_o = lambda a: (o_local(a).start(), peers(lambda p: o_copy(a, p).start()))
    send_o(2)
    own_k[:, head_of(me)] = gxk_s[slot_of(me), :]
    own_v[:, head_of(me)] = gxv_s[slot_of(me), :]
    peers(lambda p: (gx_wait(0, p).wait_recv(), gx_wait(1, p).wait_recv()))
    lpart[...] = mm_nt(own_k[...], wxk[...]) + mm_nt(own_v[...], wxv[...])

    def r_copy(w):
        return remote(lpart.at[:, cut_of(w)], lpart_in.at[vi], r_send.at[w], r_recv.at[vi], me, w)

    def r_wait(w):
        return remote(lpart.at[:, cut_of(w)], lpart_in.at[w], r_send.at[w], r_recv.at[w], me, w)

    mates(lambda w: r_copy(w).start())
    lpart_in[vi] = lpart[:, cut_of(vi)]
    mates(lambda w: r_wait(w).wait_recv())
    summed = lpart_in[0]
    for w in range(1, nv):
        summed = summed + lpart_in[w]
    glat_out[0] = summed.astype(BF16)

    def finish(p):
        lat_wait(p).wait_send()
        for a in range(5):
            in_wait(a, p).wait_send()
            o_wait(a, p).wait()
        for a in range(2):
            x_wait(a, p).wait_send()
            gx_wait(a, p).wait_send()

    peers(finish)

    def finish_mate(w):
        p_wait(w).wait_send()
        l_wait(w).wait_send()
        r_wait(w).wait_send()

    mates(finish_mate)
    for a in range(5):
        o_local(a).wait()


def by_head(nc, nv, *args):
    (feat, lat0, fgain, lgain, wq, wk, wv, wo, xwk, xwv, slot_image, segments, latest_image,
     cross_query, self_query, self_key, self_value, cross_gate, grad_output) = args
    rows, cols = self_query.shape
    total = rows * nc
    slots, wide = lat0.shape
    xrows = nc * slots
    cut = wide // nv
    vmem = pl.BlockSpec(memory_space=pltpu.VMEM)
    hbm = pl.BlockSpec(memory_space=pltpu.HBM)
    tok = jax.ShapeDtypeStruct((rows, cols), BF16)
    lat_t = jax.ShapeDtypeStruct((1, slots, cut), BF16)
    V = pltpu.VMEM
    dma = pltpu.SemaphoreType.DMA
    scratch = (
        [V((1,) + feat.shape[1:], BF16), V((slots, wide), BF16)]
        + [V((wide // 128, 128), F32)] * 2
        + [V(wq.shape, BF16)] * 3
        + [V(wo.shape, BF16)]
        + [V((1, nc), jnp.int32), V((1, total), jnp.int32), V((1, nc), F32)]
        + [V((total, DH), BF16)] * 5
        + [V((wide, cols), BF16)] * 2
        + [V((nc, 1, rows), jnp.int32)] + [V((total, 128), F32)] * 2
        + [V((slots, wide), F32), V((nv, slots, cut), F32)]
        + [V((slots, cut), BF16), V((nv, slots, cut), BF16)]
        + [V((slots, cols), BF16)] * 2
        + [V((xrows, DH), BF16)] * 2
        + [V((total, DH), BF16), V((total, xrows), F32)]
        + [V((total, total), F32)] + [V((total, DH), F32)] * 2
        + [V((total, DH), F32)] * 2
        + [V((total, DH), BF16)] * 5
        + [V((xrows, DH), F32)] * 2
        + [V((xrows, DH), BF16)] * 2
        + [V((slots, cols), BF16)] * 2
        + [V((slots, wide), F32), V((nv, slots, cut), F32)]
        + [dma((14,)), dma((5,))]
        + [dma((5, nc))] * 2
        + [dma((nc,))] * 2
        + [dma((nv,))] * 4
        + [dma((2, nc))] * 2
        + [dma((5,))]
        + [dma((5, nc))] * 2
        + [dma((2, nc))] * 2
        + [dma((nv,))] * 2
    )
    got = pl.pallas_call(
        functools.partial(head_kernel, nc, nv),
        out_shape=[tok] * 5 + [lat_t],
        in_specs=[hbm] * 19,
        out_specs=[hbm] * 5 + [vmem],
        scratch_shapes=scratch,
        compiler_params=pltpu.CompilerParams(
            collective_id=0, has_side_effects=True, vmem_limit_bytes=62 * 1024 * 1024
        ),
        name="head_window",
    )(feat, lat0, fgain.reshape(-1, 128), lgain.reshape(-1, 128), wq, wk, wv, wo, xwk, xwv, slot_image[None],
      segments[None], latest_image[None], cross_gate[None], cross_query, self_query, self_key,
      self_value, grad_output)
    moved = pl.pallas_call(
        copy_kernel,
        out_shape=[tok] * 5 + [lat_t],
        in_specs=[hbm] * 6,
        out_specs=[hbm] * 6,
        scratch_shapes=[V(t.shape, BF16) for t in [tok] * 5 + [lat_t]] + [dma((2, 6))],
        name="results",
    )(*got)
    return moved


def copy_kernel(*refs):
    n = (len(refs) - 1) // 3
    src, dst, held, sem = refs[:n], refs[n : 2 * n], refs[2 * n : 3 * n], refs[3 * n]
    first = [pltpu.make_async_copy(src[a], held[a], sem.at[0, a]) for a in range(n)]
    second = [pltpu.make_async_copy(held[a], dst[a], sem.at[1, a]) for a in range(n)]
    for c in first:
        c.start()
    for a in range(n):
        first[a].wait()
        second[a].start()
    for c in second:
        c.wait()


def dispatch(nc, nv, *args):
    if args[17].shape[0] == nc and args[0].shape[0] == 1:
        return tuple(by_head(nc, nv, *args))
    return shards(*args)


def solution(mesh):
    in_specs = (
        P("ctx", None, None),
        P(),
        P(),
        P(),
        P(None, "vis"),
        P(None, "vis"),
        P(None, "vis"),
        P("vis", None),
        P(None, "vis"),
        P(None, "vis"),
        P(),
        P(),
        P("ctx"),
        P("ctx", "vis"),
        P("ctx", "vis"),
        P("ctx", "vis"),
        P("ctx", "vis"),
        P("vis"),
        P("ctx", "vis"),
    )
    out_specs = (
        P("ctx", "vis"),
        P("ctx", "vis"),
        P("ctx", "vis"),
        P("ctx", "vis"),
        P("ctx", "vis"),
        P("ctx", None, "vis"),
    )
    body = functools.partial(dispatch, mesh.shape["ctx"], mesh.shape["vis"])
    return jax.shard_map(body, mesh=mesh, in_specs=in_specs, out_specs=out_specs, check_vma=False)
```
